128 devices in a mesh: user: 16 (over y, x_lo, core), hist: 8 (over z, x_hi).
Axes of the slice: x: 4 (x_hi: 2, x_lo: 2; x = x_hi * 2 + x_lo), y: 4, z: 4, core: 2. Of those that a mesh axis runs over, the one named last changes fastest.
Arguments:
- cand_embed: bfloat16 [32768, 1024], P(('user', 'hist')), may hold values from -6 to 6
- cand_group: int32 [32768, 1], P(('user', 'hist')), may hold values from 0 to 15; in each aligned block of 256 rows (0 to 255, 256 to 511, ...) at most 32 rows name the same one
- cand_user: int32 [32768], P(('user', 'hist')), may hold values from 0 to 3
- hist_len: int32 [64], P('user'), may hold values from 128 to 2048
- block_list: int32 [1024], P(('user', 'hist')), may hold values from 0 to 63, as said below
- hist_keys: bfloat16 [131072, 1024], P(('user', 'hist')), may hold values from -6 to 6
- hist_values: bfloat16 [131072, 1024], P(('user', 'hist')), may hold values from -6 to 6
- in_gain: float32 [1024], replicated, may hold values from 0.1 to 1.9
- w_in: bfloat16 [1024, 2048], replicated, may hold values from -0.1875 to 0.1875
- attn_gain: float32 [1024], replicated, may hold values from 0.1 to 1.9
- w_out: bfloat16 [1024, 1024], replicated, may hold values from -0.1875 to 0.1875
Outputs:
- ranked: bfloat16 [32768, 1024], P(('user', 'hist'))
The draws below stay inside these ranges and needn't reach their ends.
Inputs may be any that keep to these rules, and one draw needn't show every extreme that they name: `cand_group`: among the 256 candidates of one device at most 32 name the same group. `block_list`: each aligned run of 64 entries, one group's blocks, holds every slot of 0 to 63 once.
All inputs are finite; a program needn't handle non-finite values.
Results may differ from the reference program's by a relative error of at most 0.0059.
Values may be sent and summed in bfloat16 or wider, within the bound.
No kernel may reach another device: no remote copies, remote signals or barrier semaphores. Data moves between devices by JAX's collectives and lax.ppermute only.
A program may use at most 192 MiB of HBM per device.

```python
import math
import jax
import jax.numpy as jnp
import numpy as np
from jax import lax

D = 1024
HEADS = 8
CAND_DEV = 256
CAP = 32
USR_GRP = 4
BLK = 128
BLK_GRP = 64
BLK_USR = 16
HMAX = 2048
USERS = 64
CANDS = 32768
NBLK = 1024
HKEYS = 131072
N_USER = 16
DEVICES = 128


def draw_hist_len(key, part):
    key = jax.random.fold_in(key, 11)
    first_key, second_key, third_key = jax.random.split(key, 3)
    lengths_drawn = jax.random.randint(first_key, (USERS,), BLK, HMAX + 1)
    longest_user = jax.random.randint(second_key, (), 0, USERS)
    shortest_user = (longest_user + 1 + jax.random.randint(third_key, (), 0, USERS - 1)) % USERS
    lengths_drawn = lengths_drawn.at[shortest_user].set(BLK)
    lengths_drawn = lengths_drawn.at[longest_user].set(HMAX)
    return lengths_drawn.astype(jnp.int32)


def draw_block_list(key, part):
    key = jax.random.fold_in(key, 23)
    group_keys = jax.random.split(key, N_USER)
    orders = jax.vmap(lambda group_key: jax.random.permutation(group_key, BLK_GRP))(group_keys)
    return orders.reshape(-1).astype(jnp.int32)


def place_ends(array, stream_key, low, largest):
    place = [jax.random.randint(jax.random.fold_in(stream_key, axis), (), 0, length) for axis, length in enumerate(array.shape)]
    longest = array.shape.index(max(array.shape))
    next_to = place[:longest] + [(place[longest] + 1) % array.shape[longest]] + place[longest + 1:]
    return array.at[tuple(place)].set(low).at[tuple(next_to)].set(largest)


def block_levels(own_key, extent, cuts, least, largest):
    gain = 1.0
    for dim, shards_of in cuts:
        draws = jax.random.uniform(jax.random.fold_in(jax.random.fold_in(own_key, 6), dim), (shards_of,), jnp.float32, least / len(cuts), largest / len(cuts))
        gain = gain * jnp.repeat(jnp.exp(draws), extent[dim] // shards_of).reshape((-1,) + (1,) * (len(extent) - 1 - dim))
    return gain


def assign_block(key, own, number, rows, number_of, top, reach, lean):
    ranking = jax.random.permutation(key, number_of)
    packed, ordinary = shares(number_of, rows * top, reach, lean, True), shares(number_of, rows * top, reach, lean, False)
    places = jnp.arange(number_of)

    def named(tallies, offset_by):
        used = int((tallies > 0).sum())
        fixed = max(1, used // 4)
        passed = fixed + (places - fixed + offset_by * (used - fixed)) % max(1, number_of - fixed)
        return jnp.zeros((number_of,), jnp.int32).at[ranking[jnp.where(places < fixed, places, passed)]].set(jnp.asarray(tallies, jnp.int32))

    tallies = jnp.where(number % 4 == 0, named(packed, number // 4), named(ordinary, number - number // 4 - 1))
    mixed = jax.random.permutation(jax.random.fold_in(own, 3), number_of)
    source_of, receiver = mixed[0:number_of // 2 * 2:2], mixed[1:number_of // 2 * 2:2]
    room = jnp.minimum(tallies[source_of] - 1, reach - tallies[receiver]) // 2
    room = jnp.where((source_of == ranking[0]) | (receiver == ranking[0]) | (tallies[receiver] == 0), 0, jnp.maximum(room, 0))
    passed = jax.random.randint(jax.random.fold_in(own, 4), (number_of // 2,), 0, 1 << 20) % (room + 1)
    tallies = tallies.at[source_of].add(-passed).at[receiver].add(passed)
    members = jnp.searchsorted(jnp.cumsum(tallies), jnp.arange(rows * top), side="right").astype(jnp.int32)
    table = members.reshape(top, rows).T
    table = table[jax.random.permutation(jax.random.fold_in(own, 1), rows)]
    offset_by = jax.random.randint(jax.random.fold_in(own, 2), (rows, 1), 0, top)
    return jnp.take_along_axis(table, (jnp.arange(top)[None, :] + offset_by) % top, axis=1)


def shares(count, total, limit, skew, full):
    portions = [(1 << 20) // math.isqrt(rank ** skew) + 1 for rank in range(1, count + 1)]
    largest = limit if full else min(limit, max(-(-total // count), total * portions[0] // sum(portions)))
    least = 1 if total - largest >= count - 1 else 0
    given, surplus = [largest] + [least] * (count - 1), total - largest - least * (count - 1)
    while surplus > 0:
        free = [i for i in range(1, count) if given[i] < largest] or [i for i in range(1, count) if given[i] < limit]
        whole, remaining = sum([portions[i] for i in free]), surplus
        for i in free:
            extra = min(limit - given[i], max(1, remaining * portions[i] // whole), surplus)
            given[i] = given[i] + extra
            surplus = surplus - extra
    return np.array(given)


def normal_values(key, extent, scale, bound, cuts=(), kind=jnp.bfloat16):
    loudness = block_levels(key, extent, cuts, -0.22, 0.18) if cuts else 1.0
    drawn = jax.random.normal(key, extent, jnp.float32) * scale * loudness
    return jnp.minimum(jnp.maximum(drawn, -bound), bound).astype(kind)


def setup_inputs(seed: int = 0) -> dict:
    arg_keys = jax.random.split(jax.random.key(seed), 12)
    cand_embed = normal_values(arg_keys[0], (CANDS, D), 1.0, 6.0, ((0, 128),))
    cand_group_keys = jax.random.split(jax.random.fold_in(arg_keys[1], 1), CANDS // CAND_DEV)
    cand_group_turns = jax.random.permutation(jax.random.fold_in(arg_keys[1], 3), CANDS // CAND_DEV)
    cand_group = jax.vmap(lambda own, number: assign_block(jax.random.fold_in(arg_keys[1], 2), own, number, CAND_DEV, N_USER, 1, CAP, 2))(cand_group_keys, cand_group_turns).reshape((CANDS, 1))
    cand_user = place_ends(jax.random.randint(arg_keys[2], (CANDS,), 0, USR_GRP), jax.random.fold_in(arg_keys[2], 1), 0, USR_GRP - 1).astype(jnp.int32)
    hist_len = draw_hist_len(jax.random.fold_in(arg_keys[11], 71), 0)
    block_list = draw_block_list(jax.random.fold_in(arg_keys[11], 71), 0)
    hist_keys = normal_values(arg_keys[5], (HKEYS, D), 1.0, 6.0, ((0, 128),))
    hist_values = normal_values(arg_keys[6], (HKEYS, D), 1.0, 6.0, ((0, 128),))
    in_gain = jnp.clip(1.0 + 0.18 * jax.random.normal(arg_keys[7], (D,), jnp.float32), 0.1, 1.9)
    w_in = normal_values(arg_keys[8], (D, 2 * D), D ** -0.5, 0.1875)
    attn_gain = jnp.clip(1.0 + 0.18 * jax.random.normal(arg_keys[9], (D,), jnp.float32), 0.1, 1.9)
    w_out = normal_values(arg_keys[10], (D, D), D ** -0.5, 0.1875)
    return {"cand_embed": cand_embed, "cand_group": cand_group, "cand_user": cand_user, "hist_len": hist_len, "block_list": block_list, "hist_keys": hist_keys, "hist_values": hist_values, "in_gain": in_gain, "w_in": w_in, "attn_gain": attn_gain, "w_out": w_out}


def prepare(embed, in_gain, w_in):
    values_full = embed.astype(jnp.float32)
    scaling = lax.rsqrt(lax.optimization_barrier(jnp.mean(values_full * values_full, axis=-1, keepdims=True)) + 1e-06)
    normed = (values_full * scaling * in_gain).astype(jnp.bfloat16)
    projected = jax.nn.silu(jnp.dot(normed, w_in, preferred_element_type=jnp.float32))
    model_width = embed.shape[1]
    return (projected[:, :model_width].astype(jnp.bfloat16), projected[:, model_width:].astype(jnp.bfloat16))

def finish(embed, attended, gate_u, attn_gain, w_out):
    scaling = lax.rsqrt(lax.optimization_barrier(jnp.mean(attended * attended, axis=-1, keepdims=True)) + 1e-05)
    gated = (attended * scaling * attn_gain * gate_u.astype(jnp.float32)).astype(jnp.bfloat16)
    mixed = embed.astype(jnp.float32) + jnp.dot(gated, w_out, preferred_element_type=jnp.float32)
    return mixed.astype(jnp.bfloat16)

def attend(queries, query_tags, keys, values, key_tags):
    query_rows, model_width = queries.shape
    key_rows = keys.shape[0]
    query_block = 512 if query_rows % 512 == 0 else query_rows
    key_block = 1024 if key_rows % 1024 == 0 else key_rows
    head_size = model_width // HEADS
    scale = head_size ** (-0.5)
    key_parts = (keys.reshape(key_rows // key_block, key_block, HEADS, head_size), values.reshape(key_rows // key_block, key_block, HEADS, head_size), key_tags.reshape(key_rows // key_block, key_block))

    def per_query(block):
        query_part, tag_part = block
        query_heads = query_part.reshape(query_block, HEADS, head_size).astype(jnp.float32)

        def step(running, key_part):
            key_heads, value_heads, tag_keys = key_part
            scores = jnp.einsum('qhd,khd->hqk', query_heads, key_heads.astype(jnp.float32)) * scale
            visible = tag_part[:, None] == tag_keys[None, :]
            weights = jnp.where(visible[None], jax.nn.silu(scores), 0.0).astype(jnp.bfloat16)
            outputs = jnp.einsum('hqk,khd->qhd', weights.astype(jnp.float32), value_heads.astype(jnp.float32))
            return (running + outputs.reshape(query_block, model_width), None)
        running, unused = lax.scan(step, jnp.zeros((query_block, model_width), jnp.float32), key_parts)
        return running
    result = lax.map(per_query, (queries.reshape(query_rows // query_block, query_block, model_width), query_tags.reshape(query_rows // query_block, query_block)))
    return result.reshape(query_rows, model_width)

def reference(cand_embed, cand_group, cand_user, hist_len, block_list, hist_keys, hist_values, in_gain, w_in, attn_gain, w_out):
    query, gate_u = prepare(cand_embed, in_gain, w_in)
    target_group = cand_group[:, 0]
    member = (target_group[:, None] == jnp.arange(N_USER, dtype=jnp.int32)[None, :]).astype(jnp.int32)
    member = member.reshape(DEVICES, CAND_DEV, N_USER)
    position = (lax.optimization_barrier(jnp.sum(jnp.cumsum(member, axis=1) * member, axis=-1)) - 1).reshape(-1)
    source = jnp.arange(CANDS, dtype=jnp.int32) // CAND_DEV
    target_slot = (source * CAP + position).astype(jnp.int32)
    query_buffer = jnp.zeros((N_USER, DEVICES * CAP, D), jnp.bfloat16).at[target_group, target_slot].set(query)
    tag_buffer = jnp.full((N_USER, DEVICES * CAP), USR_GRP, jnp.bfloat16).at[target_group, target_slot].set(cand_user.astype(jnp.bfloat16))
    owner_user = block_list // BLK_USR
    block_rank = block_list % BLK_USR
    block_group = jnp.arange(NBLK, dtype=jnp.int32) // BLK_GRP
    length_of = hist_len[(block_group * USR_GRP + owner_user).astype(jnp.int32)]
    offsets = block_rank[:, None] * BLK + jnp.arange(BLK, dtype=jnp.int32)[None, :]
    key_tags = jnp.where(offsets < length_of[:, None], owner_user[:, None], -1)
    key_tags = key_tags.reshape(N_USER, BLK_GRP * BLK).astype(jnp.bfloat16)
    group_keys = hist_keys.reshape(N_USER, BLK_GRP * BLK, D)
    group_values = hist_values.reshape(N_USER, BLK_GRP * BLK, D)

    def per_group(items):
        return attend(items[0], items[1], items[2], items[3], items[4])
    attended_all = lax.map(per_group, (query_buffer, tag_buffer, group_keys, group_values, key_tags))
    attended = attended_all[target_group, target_slot]
    return finish(cand_embed, attended, gate_u, attn_gain, w_out)
```

```python
import functools

import jax
import jax.numpy as jnp
from jax import lax
from jax.experimental import pallas as pl
from jax.experimental.pallas import tpu as pltpu
from jax.sharding import PartitionSpec as P

HEADS = 8
HEAD = 128
BLK = 128
BLK_USR = 16
USERS = 4
SLOTS = 32
CHUNK = 512
PAD = 16
SORTED = CHUNK + USERS * PAD
TILE = 256
KEYS = 256
VMEM = 48 * 1024 * 1024

BF16 = jnp.bfloat16
F32 = jnp.float32


def dot(a, b, contract):
    return lax.dot_general(a, b, ((contract[0], contract[1]), ((), ())), preferred_element_type=F32)


def params():
    return pltpu.CompilerParams(vmem_limit_bytes=VMEM)


def vmem():
    return pl.BlockSpec(memory_space=pltpu.VMEM)


def smem():
    return pl.BlockSpec(memory_space=pltpu.SMEM)


def regroup_kernel(list_ref, keys_ref, values_ref, out_ref):
    rows = keys_ref.shape[0]
    out_ref[0, :rows, :HEAD] = keys_ref[...]
    out_ref[0, :rows, HEAD:] = values_ref[...]
    out_ref[0, rows:, :] = jnp.broadcast_to(list_ref[...], (PAD, 2 * HEAD)).astype(BF16)


def regroup(block_list, keys, values):
    rows = keys.shape[0]
    listed = jnp.pad(block_list, (0, 2 * HEAD - block_list.shape[0])).reshape(1, -1)
    return pl.pallas_call(
        regroup_kernel,
        grid=(HEADS,),
        out_shape=jax.ShapeDtypeStruct((HEADS, rows + PAD, 2 * HEAD), BF16),
        in_specs=[
            pl.BlockSpec((1, 2 * HEAD), lambda h: (0, 0)),
            pl.BlockSpec((rows, HEAD), lambda h: (0, h)),
            pl.BlockSpec((rows, HEAD), lambda h: (0, h)),
        ],
        out_specs=pl.BlockSpec((1, rows + PAD, 2 * HEAD), lambda h: (h, 0, 0)),
        compiler_params=params(),
        name="regroup",
    )(listed, keys, values)


def prepare_kernel(
    turn_ref, group_ref, user_ref, embed_ref, gain_ref, w_ref, packed_ref, gate_ref, slot_ref
):
    rows, width = embed_ref.shape
    groups = packed_ref.shape[0]
    slots = groups * SLOTS
    group = group_ref[...]
    lane = lax.broadcasted_iota(jnp.int32, (rows, HEAD), 1)
    member = (group == lane).astype(F32)
    before = (
        lax.broadcasted_iota(jnp.int32, (rows, rows), 1)
        < lax.broadcasted_iota(jnp.int32, (rows, rows), 0)
    ).astype(BF16)
    count = dot(before, member.astype(BF16), ((1,), (0,)))
    position = jnp.sum(count * member, axis=1, keepdims=True).astype(jnp.int32)
    slot = group * SLOTS + position
    slot_ref[...] = slot
    offset = turn_ref[0] * SLOTS
    users = jnp.where(lane == position + offset, (user_ref[...] - USERS).astype(F32), 0.0)
    own = lax.broadcasted_iota(jnp.int32, (HEAD, HEAD), 1) - offset
    tags = dot(member.astype(BF16), users.astype(BF16), ((0,), (0,)))
    tags = tags + jnp.where((own >= 0) & (own < SLOTS), USERS, 0).astype(F32)
    tags = tags[:groups].reshape(groups, 1, HEAD)
    tags = jnp.broadcast_to(tags, (groups, PAD, HEAD)).astype(BF16)

    values = embed_ref[...].astype(F32)
    scaling = lax.rsqrt(jnp.mean(values * values, axis=-1, keepdims=True) + 1e-06)
    normed = (values * scaling * gain_ref[...]).astype(BF16)
    place = (slot == lax.broadcasted_iota(jnp.int32, (rows, slots), 1)).astype(BF16)
    query = dot(normed, w_ref[:, :width], ((1,), (0,)))
    query = (query / (1.0 + jnp.exp(-query))).astype(BF16)
    packed = dot(place, query, ((0,), (0,))).astype(BF16)
    for h in range(HEADS):
        packed_ref[:, h, :SLOTS] = packed[:, h * HEAD : (h + 1) * HEAD].reshape(
            groups, SLOTS, HEAD
        )
        packed_ref[:, h, SLOTS:] = tags
    gate = dot(normed, w_ref[:, width:], ((1,), (0,)))
    gate_ref[...] = (gate / (1.0 + jnp.exp(-gate))).astype(BF16)


def prepare(turn, group, user, embed, gain, w_in, groups):
    rows, width = embed.shape
    return pl.pallas_call(
        prepare_kernel,
        out_shape=(
            jax.ShapeDtypeStruct((groups, HEADS, SLOTS + PAD, HEAD), BF16),
            jax.ShapeDtypeStruct((rows, width), BF16),
            jax.ShapeDtypeStruct((rows, 1), jnp.int32),
        ),
        in_specs=[smem()] + [vmem()] * 5,
        out_specs=(vmem(), vmem(), vmem()),
        compiler_params=params(),
        name="prepare",
    )(turn, group, user, embed, gain.reshape(1, width), w_in)


def padded(count):
    return (count + (PAD - 1)) // PAD * PAD


def bases(counts_ref, chunks):
    starts, sizes, start = [], [], jnp.int32(0)
    for u in range(USERS):
        size = jnp.int32(0)
        for c in range(chunks):
            size = size + padded(counts_ref[c, u])
        starts.append(start)
        sizes.append(size)
        start = start + size
    return starts, sizes


def copy_rows(count, load, store):
    def step(i, carry):
        at = pl.multiple_of(i * PAD, PAD)
        store(at, load(at))
        return carry

    lax.fori_loop(0, padded(count) // PAD, step, 0)


def sort_kernel(counts_ref, tags_ref, query_ref, place_ref, sorted_ref, chunk_ref):
    chunks = tags_ref.shape[0]
    sources = CHUNK // SLOTS
    next_rows, _ = bases(counts_ref, chunks)
    earlier = (
        lax.broadcasted_iota(jnp.int32, (CHUNK, CHUNK), 0)
        < lax.broadcasted_iota(jnp.int32, (CHUNK, CHUNK), 1)
    ).astype(BF16)
    for c in range(chunks):
        tags = tags_ref[c : c + 1, :]
        lanes = (tags == lax.broadcasted_iota(jnp.int32, (8, CHUNK), 0)).astype(F32)
        rank = dot(lanes.astype(BF16), earlier, ((1,), (0,))).astype(jnp.int32)
        start = jnp.int32(0)
        starts = []
        place = jnp.full((1, CHUNK), -1, jnp.int32)
        for u in range(USERS):
            place = jnp.where(tags == u, rank[u : u + 1, :] + start, place)
            starts.append(start)
            start = start + padded(counts_ref[c, u])
        place_ref[c : c + 1, :] = place
        pick = (lax.broadcasted_iota(jnp.int32, (SORTED, CHUNK), 0) == place).astype(BF16)
        query = query_ref[c * sources : (c + 1) * sources, :SLOTS].reshape(CHUNK, HEAD)
        chunk_ref[...] = dot(pick, query, ((1,), (0,))).astype(BF16)
        for u in range(USERS):
            source, target = starts[u], next_rows[u]

            def load(at, source=source):
                return chunk_ref[pl.ds(pl.multiple_of(source + at, PAD), PAD), :]

            def store(at, rows, target=target):
                sorted_ref[pl.ds(pl.multiple_of(target + at, PAD), PAD), :] = rows

            copy_rows(counts_ref[c, u], load, store)
            next_rows[u] = next_rows[u] + padded(counts_ref[c, u])


def sort_queries(counts, tags, query):
    chunks = tags.shape[0]
    return pl.pallas_call(
        sort_kernel,
        out_shape=(
            jax.ShapeDtypeStruct((chunks, CHUNK), jnp.int32),
            jax.ShapeDtypeStruct((chunks * SORTED + TILE, HEAD), BF16),
        ),
        in_specs=[smem(), vmem(), vmem()],
        out_specs=(vmem(), vmem()),
        scratch_shapes=[pltpu.VMEM((SORTED, HEAD), BF16)],
        compiler_params=params(),
        name="sort_queries",
    )(counts, tags, query)


def attend_kernel(
    counts_ref, where_ref, length_ref, place_ref, query_ref, kv_ref, out_ref, kv, total, chunk, sems
):
    chunks = out_ref.shape[0]
    blocks = kv_ref.shape[1] // BLK
    starts, sizes = bases(counts_ref, chunks)

    def fetch(u, r):
        slot = u * BLK_USR + r
        at = where_ref[slot]
        return pltpu.make_async_copy(
            kv_ref.at[at // blocks, pl.ds(pl.multiple_of(at % blocks * BLK, BLK), BLK), :],
            kv.at[pl.ds(pl.multiple_of(slot * BLK, BLK), BLK), :],
            sems.at[slot],
        )

    steps = []
    for u in range(USERS):
        step_count = (length_ref[u] + (KEYS - 1)) // KEYS
        steps.append(step_count)

        def begin(r, carry, u=u):
            fetch(u, r).start()
            return carry

        lax.fori_loop(0, step_count * (KEYS // BLK), begin, 0)

    scale = 0.5 * HEAD ** (-0.5)
    for u in range(USERS):

        def finish(r, carry, u=u):
            fetch(u, r).wait()
            return carry

        lax.fori_loop(0, steps[u] * (KEYS // BLK), finish, 0)

        def tile(i, carry, u=u):
            at = pl.multiple_of(starts[u] + i * TILE, PAD)
            query = query_ref[pl.ds(at, TILE), :]

            def step(k, running):
                row = pl.multiple_of(u * BLK_USR * BLK + k * KEYS, KEYS)
                half = dot(query, kv[pl.ds(row, KEYS), :HEAD], ((1,), (1,))) * scale
                weight = half + half * jnp.tanh(half)
                column = lax.broadcasted_iota(jnp.int32, (TILE, KEYS), 1)
                weight = jnp.where(column < length_ref[u] - k * KEYS, weight, 0.0)
                return running + dot(weight.astype(BF16), kv[pl.ds(row, KEYS), HEAD:], ((1,), (0,)))

            running = lax.fori_loop(0, steps[u], step, jnp.zeros((TILE, HEAD), F32))
            total[pl.ds(at, TILE), :] = running.astype(BF16)
            return carry

        lax.fori_loop(0, (sizes[u] + (TILE - 1)) // TILE, tile, 0)

    next_rows = list(starts)
    for c in range(chunks):
        chunk[...] = jnp.zeros_like(chunk)
        start = jnp.int32(0)
        for u in range(USERS):
            source, target = next_rows[u], start

            def load(at, source=source):
                return total[pl.ds(pl.multiple_of(source + at, PAD), PAD), :]

            def store(at, rows, target=target):
                chunk[pl.ds(pl.multiple_of(target + at, PAD), PAD), :] = rows

            copy_rows(counts_ref[c, u], load, store)
            start = start + padded(counts_ref[c, u])
            next_rows[u] = next_rows[u] + padded(counts_ref[c, u])
        place = place_ref[c : c + 1, :]
        pick = (lax.broadcasted_iota(jnp.int32, (SORTED, CHUNK), 0) == place).astype(BF16)
        out_ref[c] = dot(pick, chunk[...], ((0,), (0,))).astype(BF16)


def attend(counts, where, length, place, query, kv):
    chunks = place.shape[0]
    rows = query.shape[0]
    blocks = USERS * BLK_USR
    return pl.pallas_call(
        attend_kernel,
        out_shape=jax.ShapeDtypeStruct((chunks, CHUNK, HEAD), BF16),
        in_specs=[smem(), smem(), smem(), vmem(), vmem(), pl.BlockSpec(memory_space=pl.ANY)],
        out_specs=vmem(),
        scratch_shapes=[
            pltpu.VMEM((blocks * BLK, 2 * HEAD), BF16),
            pltpu.VMEM((rows, HEAD), BF16),
            pltpu.VMEM((SORTED, HEAD), BF16),
            pltpu.SemaphoreType.DMA((blocks,)),
        ],
        compiler_params=params(),
        name="attend",
    )(counts, where, length, place, query, kv)


def finish_kernel(returned_ref, slot_ref, embed_ref, gate_ref, gain_ref, w_ref, out_ref, attended):
    rows, width = embed_ref.shape
    slots = returned_ref.shape[0] * SLOTS
    place = (slot_ref[...] == lax.broadcasted_iota(jnp.int32, (rows, slots), 1)).astype(BF16)
    for h in range(HEADS):
        attended[:, h * HEAD : (h + 1) * HEAD] = dot(
            place, returned_ref[:, h].reshape(slots, HEAD), ((1,), (0,))
        )
    picked = attended[...]
    scaling = lax.rsqrt(jnp.mean(picked * picked, axis=-1, keepdims=True) + 1e-05)
    gated = (picked * scaling * gain_ref[...] * gate_ref[...].astype(F32)).astype(BF16)
    mixed = embed_ref[...].astype(F32) + dot(gated, w_ref[...], ((1,), (0,)))
    out_ref[...] = mixed.astype(BF16)


def finish(returned, slot, embed, gate, gain, w_out):
    rows, width = embed.shape
    return pl.pallas_call(
        finish_kernel,
        out_shape=jax.ShapeDtypeStruct((rows, width), BF16),
        in_specs=[vmem()] * 6,
        out_specs=vmem(),
        scratch_shapes=[pltpu.VMEM((rows, width), F32)],
        compiler_params=params(),
        name="finish",
    )(returned, slot, embed, gate, gain.reshape(1, width), w_out)


def body(
    cand_embed,
    cand_group,
    cand_user,
    hist_len,
    block_list,
    hist_keys,
    hist_values,
    in_gain,
    w_in,
    attn_gain,
    w_out,
):
    groups = lax.axis_size("user")
    hist_count = lax.axis_size("hist")
    devices = groups * hist_count
    everyone = ("user", "hist")
    blocks_here = block_list.shape[0]

    kv = regroup(block_list, hist_keys, hist_values)
    kv, embed = lax.optimization_barrier((kv, cand_embed))
    kv = lax.all_to_all(kv, "hist", split_axis=0, concat_axis=0, tiled=True)

    me = lax.axis_index("user") * hist_count + lax.axis_index("hist")
    turn = jnp.reshape(me % (HEAD // SLOTS), (1,)).astype(jnp.int32)
    packed, gate, slot = prepare(
        turn, cand_group, cand_user.reshape(-1, 1), embed, in_gain, w_in, groups
    )
    arrived = lax.all_to_all(
        packed.reshape(devices, SLOTS + PAD, HEAD),
        everyone,
        split_axis=0,
        concat_axis=0,
        tiled=True,
    )

    tags = arrived[:, SLOTS, :].astype(jnp.int32).reshape(-1, HEAD // SLOTS, HEAD)
    tags = jnp.sum(tags, axis=1).reshape(devices * SLOTS // CHUNK, CHUNK)
    counts = jnp.sum(
        tags[:, None, :] == jnp.arange(USERS, dtype=jnp.int32)[None, :, None],
        axis=2,
        dtype=jnp.int32,
    )
    listed = kv[:, -1, :blocks_here].astype(jnp.int32).reshape(1, -1)
    order = jnp.arange(hist_count * blocks_here, dtype=jnp.int32)
    where = jnp.sum(jnp.where(listed == order[:, None], order[None, :], 0), axis=1)

    place, query = sort_queries(counts, tags, arrived)
    attended = attend(counts, where, hist_len, place, query, kv)
    returned = lax.all_to_all(
        attended.reshape(devices, SLOTS, HEAD), everyone, split_axis=0, concat_axis=0, tiled=True
    )
    return finish(
        returned.reshape(groups, HEADS, SLOTS, HEAD), slot, cand_embed, gate, attn_gain, w_out
    )


def solution(mesh):
    split = P(("user", "hist"))
    in_specs = (split, split, split, P("user"), split, split, split, P(), P(), P(), P())
    return jax.shard_map(body, mesh=mesh, in_specs=in_specs, out_specs=split, check_vma=False)
```

```python
import functools

import jax
import jax.numpy as jnp
from jax import lax
from jax.experimental import pallas as pl
from jax.experimental.pallas import tpu as pltpu
from jax.sharding import PartitionSpec as P

HEADS = 8
HEAD = 128
BLK = 128
BLK_USR = 16
USERS = 4
SLOTS = 32
CHUNK = 512
PAD = 16
SORTED = CHUNK + 128
COPY = 64
TILE = 256
KEYS = 1024
REST = 512
VMEM = 48 * 1024 * 1024

BF16 = jnp.bfloat16
F32 = jnp.float32


def dot(a, b, contract):
    return lax.dot_general(a, b, ((contract[0], contract[1]), ((), ())), preferred_element_type=F32)


def params():
    return pltpu.CompilerParams(vmem_limit_bytes=VMEM)


def vmem():
    return pl.BlockSpec(memory_space=pltpu.VMEM)


def smem():
    return pl.BlockSpec(memory_space=pltpu.SMEM)


def regroup_kernel(keys_ref, values_ref, out_ref):
    out_ref[0, :, :HEAD] = keys_ref[...]
    out_ref[0, :, HEAD:] = values_ref[...]


def regroup(keys, values):
    rows = keys.shape[0]
    return pl.pallas_call(
        regroup_kernel,
        grid=(HEADS,),
        out_shape=jax.ShapeDtypeStruct((HEADS, rows, 2 * HEAD), BF16),
        in_specs=[pl.BlockSpec((rows, HEAD), lambda h: (0, h))] * 2,
        out_specs=pl.BlockSpec((1, rows, 2 * HEAD), lambda h: (h, 0, 0)),
        compiler_params=params(),
        name="regroup",
    )(keys, values)


def query_kernel(
    turn_ref,
    list_ref,
    group_ref,
    user_ref,
    embed_ref,
    gain_ref,
    w_ref,
    packed_ref,
    normed_ref,
    slot_ref,
    place,
    notes,
):
    rows = embed_ref.shape[0]
    groups = packed_ref.shape[0]
    slots = groups * SLOTS

    @pl.when(pl.program_id(0) == 0)
    def _():
        group = group_ref[...]
        member = (group == lax.broadcasted_iota(jnp.int32, (groups, rows), 0)).astype(F32)
        before = (
            lax.broadcasted_iota(jnp.int32, (rows, rows), 0)
            < lax.broadcasted_iota(jnp.int32, (rows, rows), 1)
        ).astype(BF16)
        count = dot(member.astype(BF16), before, ((1,), (0,)))
        position = jnp.sum(count * member, axis=0, keepdims=True).astype(jnp.int32)
        slot = group * SLOTS + position
        slot_ref[...] = slot
        place[...] = (slot == lax.broadcasted_iota(jnp.int32, (slots, rows), 0)).astype(BF16)
        offset = turn_ref[0] * SLOTS
        lanes = lax.broadcasted_iota(jnp.int32, (HEAD, rows), 0) == position + offset
        users = member * (user_ref[...] - USERS).astype(F32)
        tags = dot(users.astype(BF16), lanes.astype(BF16), ((1,), (1,)))
        own = lax.broadcasted_iota(jnp.int32, tags.shape, 1) - offset
        tags = tags + jnp.where((own >= 0) & (own < SLOTS), USERS, 0).astype(F32)
        lane = lax.broadcasted_iota(jnp.int32, (groups, PAD, HEAD), 2)
        row = lax.broadcasted_iota(jnp.int32, (groups, PAD, HEAD), 1)
        listed = jnp.zeros((groups, PAD, HEAD), jnp.int32)
        for b in range(list_ref.shape[0]):
            listed = jnp.where(lane == b, list_ref[b], listed)
        tags = jnp.broadcast_to(tags.reshape(groups, 1, HEAD), (groups, PAD, HEAD))
        notes[...] = jnp.where(
            row == 0, tags, jnp.where(row == 1, listed.astype(F32), 0.0)
        ).astype(BF16)
        values = embed_ref[...].astype(F32)
        scaling = lax.rsqrt(jnp.mean(values * values, axis=-1, keepdims=True) + 1e-06)
        normed_ref[...] = (values * scaling * gain_ref[...]).astype(BF16)

    query = dot(normed_ref[...], w_ref[...], ((1,), (0,)))
    query = (query / (1.0 + jnp.exp(-query))).astype(BF16)
    packed = dot(place[...], query, ((1,), (0,))).astype(BF16)
    for h in range(packed_ref.shape[1]):
        packed_ref[:, h, :SLOTS] = packed[:, h * HEAD : (h + 1) * HEAD].reshape(
            groups, SLOTS, HEAD
        )
        packed_ref[:, h, SLOTS:] = notes[...]


def make_queries(turn, listed, group, user, embed, gain, w_in, groups):
    rows, width = embed.shape
    step = 2 * HEAD

    def whole(*shape):
        return pl.BlockSpec(shape, lambda i: (0,) * len(shape))

    return pl.pallas_call(
        query_kernel,
        grid=(width // step,),
        out_shape=(
            jax.ShapeDtypeStruct((groups, HEADS, SLOTS + PAD, HEAD), BF16),
            jax.ShapeDtypeStruct((rows, width), BF16),
            jax.ShapeDtypeStruct((1, rows), jnp.int32),
        ),
        in_specs=[
            smem(),
            smem(),
            whole(1, rows),
            whole(1, rows),
            whole(rows, width),
            whole(1, width),
            pl.BlockSpec((width, step), lambda i: (0, i)),
        ],
        out_specs=(
            pl.BlockSpec((groups, step // HEAD, SLOTS + PAD, HEAD), lambda i: (0, i, 0, 0)),
            whole(rows, width),
            whole(1, rows),
        ),
        scratch_shapes=[
            pltpu.VMEM((groups * SLOTS, rows), BF16),
            pltpu.VMEM((groups, PAD, HEAD), BF16),
        ],
        compiler_params=params(),
        name="make_queries",
    )(turn, listed, group, user, embed, gain.reshape(1, width), w_in)


def gate_kernel(slot_ref, normed_ref, w_ref, gate_ref, place_ref):
    rows = normed_ref.shape[0]
    gate = dot(normed_ref[...], w_ref[...], ((1,), (0,)))
    gate_ref[...] = (gate / (1.0 + jnp.exp(-gate))).astype(BF16)
    column = jnp.broadcast_to(slot_ref[...].astype(F32), (8, rows)).T[:, :1].astype(jnp.int32)
    lane = lax.broadcasted_iota(jnp.int32, place_ref.shape, 1)
    place_ref[...] = (column == lane).astype(BF16)


def make_gate(slot, normed, w_in, slots):
    rows, width = normed.shape
    return pl.pallas_call(
        gate_kernel,
        grid=(1,),
        out_shape=(
            jax.ShapeDtypeStruct((rows, width), BF16),
            jax.ShapeDtypeStruct((rows, slots), BF16),
        ),
        in_specs=[
            pl.BlockSpec((1, rows), lambda i: (0, 0)),
            pl.BlockSpec((rows, width), lambda i: (0, 0)),
            pl.BlockSpec((width, width), lambda i: (0, 1)),
        ],
        out_specs=(
            pl.BlockSpec((rows, width), lambda i: (0, 0)),
            pl.BlockSpec((rows, slots), lambda i: (0, 0)),
        ),
        compiler_params=params(),
        name="make_gate",
    )(slot, normed, w_in)


def padded(count):
    return (count + (PAD - 1)) // PAD * PAD


def bases(counts_ref, chunks):
    starts, sizes, start = [], [], jnp.int32(0)
    for u in range(USERS):
        size = jnp.int32(0)
        for c in range(chunks):
            size = size + padded(counts_ref[c, u])
        starts.append(start)
        sizes.append(size)
        start = start + size
    return starts, sizes


def copy_rows(count, source, start, target, end):
    def step(i, carry):
        rows = source[pl.ds(pl.multiple_of(start + i * COPY, PAD), COPY), :]
        target[pl.ds(pl.multiple_of(end + i * COPY, PAD), COPY), :] = rows
        return carry

    lax.fori_loop(0, (count + (COPY - 1)) // COPY, step, 0)


def runs(counts_ref, c):
    starts, start = [], jnp.int32(0)
    for u in range(USERS):
        starts.append(start)
        start = start + padded(counts_ref[c, u])
    return starts


def sort_kernel(counts_ref, tags_ref, query_ref, pick_ref, sorted_ref, chunk_ref):
    chunks = tags_ref.shape[0]
    sources = CHUNK // SLOTS
    earlier = (
        lax.broadcasted_iota(jnp.int32, (CHUNK, CHUNK), 0)
        < lax.broadcasted_iota(jnp.int32, (CHUNK, CHUNK), 1)
    ).astype(BF16)
    places = []
    for c in range(chunks):
        tags = tags_ref[c : c + 1, :]
        lanes = (tags == lax.broadcasted_iota(jnp.int32, (8, CHUNK), 0)).astype(F32)
        rank = dot(lanes.astype(BF16), earlier, ((1,), (0,))).astype(jnp.int32)
        starts = runs(counts_ref, c)
        place = jnp.full((1, CHUNK), -1, jnp.int32)
        for u in range(USERS):
            place = jnp.where(tags == u, rank[u : u + 1, :] + starts[u], place)
        places.append(place)
        pick = (lax.broadcasted_iota(jnp.int32, (SORTED, CHUNK), 0) == place).astype(BF16)
        query = query_ref[c * sources : (c + 1) * sources, :SLOTS].reshape(CHUNK, HEAD)
        chunk_ref[c * SORTED : (c + 1) * SORTED, :] = dot(pick, query, ((1,), (0,))).astype(BF16)
    chunk_ref[chunks * SORTED :, :] = jnp.zeros((COPY, HEAD), BF16)
    sorted_ref[...] = jnp.zeros_like(sorted_ref)
    row = jnp.int32(0)
    for u in range(USERS):
        for c in range(chunks):
            count = counts_ref[c, u]
            copy_rows(count, chunk_ref, c * SORTED + runs(counts_ref, c)[u], sorted_ref, row)
            row = row + padded(count)
    columns = jnp.concatenate(places, axis=0).astype(F32).T.astype(jnp.int32)
    for c in range(chunks):
        lane = lax.broadcasted_iota(jnp.int32, (CHUNK, SORTED), 1)
        pick_ref[c] = (columns[:, c : c + 1] == lane).astype(BF16)


def sort_queries(counts, tags, query):
    chunks = tags.shape[0]
    return pl.pallas_call(
        sort_kernel,
        out_shape=(
            jax.ShapeDtypeStruct((chunks, CHUNK, SORTED), BF16),
            jax.ShapeDtypeStruct((chunks * SORTED + TILE, HEAD), BF16),
        ),
        in_specs=[smem(), vmem(), vmem()],
        out_specs=(vmem(), vmem()),
        scratch_shapes=[pltpu.VMEM((chunks * SORTED + COPY, HEAD), BF16)],
        compiler_params=params(),
        name="sort_queries",
    )(counts, tags, query)


def attend_kernel(
    counts_ref,
    where_ref,
    length_ref,
    query_ref,
    pick_hbm,
    kv_hbm,
    out_ref,
    kv,
    pick,
    total,
    chunk,
    kv_sem,
    pick_sem,
):
    chunks = out_ref.shape[0]
    blocks = kv_hbm.shape[1] // BLK
    starts, sizes = bases(counts_ref, chunks)
    fetch = pltpu.make_async_copy(kv_hbm, kv, kv_sem)
    fetch.start()
    picks = pltpu.make_async_copy(pick_hbm, pick, pick_sem)
    picks.start()
    total[...] = jnp.zeros_like(total)
    chunk[...] = jnp.zeros_like(chunk)
    fetch.wait()

    scale = 0.5 * HEAD ** (-0.5)

    def partial(query, u, first, count, limit):
        parts = []
        for j in range(count):
            at = where_ref[u * BLK_USR + first + j]
            row = pl.multiple_of(at % blocks * BLK, BLK)
            parts.append(kv[at // blocks, pl.ds(row, BLK), :])
        part = jnp.concatenate(parts, axis=0)
        half = dot(query, part[:, :HEAD], ((1,), (1,))) * scale
        weight = half + half * jnp.tanh(half)
        if limit is not None:
            column = lax.broadcasted_iota(jnp.int32, weight.shape, 1)
            weight = jnp.where(column < limit, weight, 0.0)
        return dot(weight.astype(BF16), part[:, HEAD:], ((1,), (0,)))

    for u in range(USERS):
        length = length_ref[u]
        whole = length // KEYS
        rest = (length - whole * KEYS + (REST - 1)) // REST

        def tile(i, carry, u=u, length=length, whole=whole, rest=rest):
            at = pl.multiple_of(starts[u] + i * TILE, PAD)
            query = query_ref[pl.ds(at, TILE), :]

            def step(k, running):
                return running + partial(query, u, k * (KEYS // BLK), KEYS // BLK, None)

            def end(k, running):
                first = whole * KEYS + k * REST
                return running + partial(query, u, first // BLK, REST // BLK, length - first)

            running = lax.fori_loop(0, whole, step, jnp.zeros((TILE, HEAD), F32))
            running = lax.fori_loop(0, rest, end, running)
            total[pl.ds(at, TILE), :] = running.astype(BF16)
            return carry

        lax.fori_loop(0, (sizes[u] + (TILE - 1)) // TILE, tile, 0)

    picks.wait()
    rows = list(starts)
    for c in range(chunks):
        run = runs(counts_ref, c)
        for u in range(USERS):
            count = counts_ref[c, u]
            copy_rows(count, total, rows[u], chunk, c * SORTED + run[u])
            rows[u] = rows[u] + padded(count)
    for c in range(chunks):
        out_ref[c] = dot(pick[c], chunk[c * SORTED : (c + 1) * SORTED, :], ((1,), (0,))).astype(BF16)


def attend(counts, where, length, query, pick, kv):
    chunks = pick.shape[0]
    rows = query.shape[0]
    anywhere = pl.BlockSpec(memory_space=pl.ANY)
    return pl.pallas_call(
        attend_kernel,
        out_shape=jax.ShapeDtypeStruct((chunks, CHUNK, HEAD), BF16),
        in_specs=[smem(), smem(), smem(), vmem(), anywhere, anywhere],
        out_specs=vmem(),
        scratch_shapes=[
            pltpu.VMEM(kv.shape, BF16),
            pltpu.VMEM(pick.shape, BF16),
            pltpu.VMEM((rows, HEAD), BF16),
            pltpu.VMEM((chunks * SORTED + COPY, HEAD), BF16),
            pltpu.SemaphoreType.DMA,
            pltpu.SemaphoreType.DMA,
        ],
        compiler_params=params(),
        name="attend",
    )(counts, where, length, query, pick, kv)


def finish_kernel(returned_ref, place_ref, embed_ref, gate_ref, gain_ref, w_ref, out_ref, attended):
    slots = place_ref.shape[1]
    for h in range(HEADS):
        attended[:, h * HEAD : (h + 1) * HEAD] = dot(
            place_ref[...], returned_ref[:, h].reshape(slots, HEAD), ((1,), (0,))
        )
    picked = attended[...]
    scaling = lax.rsqrt(jnp.mean(picked * picked, axis=-1, keepdims=True) + 1e-05)
    gated = (picked * scaling * gain_ref[...] * gate_ref[...].astype(F32)).astype(BF16)
    mixed = embed_ref[...].astype(F32) + dot(gated, w_ref[...], ((1,), (0,)))
    out_ref[...] = mixed.astype(BF16)


def finish(returned, place, embed, gate, gain, w_out):
    rows, width = embed.shape
    return pl.pallas_call(
        finish_kernel,
        out_shape=jax.ShapeDtypeStruct((rows, width), BF16),
        in_specs=[vmem()] * 6,
        out_specs=vmem(),
        scratch_shapes=[pltpu.VMEM((rows, width), F32)],
        compiler_params=params(),
        name="finish",
    )(returned, place, embed, gate, gain.reshape(1, width), w_out)


def body(
    cand_embed,
    cand_group,
    cand_user,
    hist_len,
    block_list,
    hist_keys,
    hist_values,
    in_gain,
    w_in,
    attn_gain,
    w_out,
):
    groups = lax.axis_size("user")
    hist_count = lax.axis_size("hist")
    devices = groups * hist_count
    everyone = ("user", "hist")
    blocks_here = block_list.shape[0]

    rows = cand_embed.shape[0]
    me_user = lax.axis_index("user")
    me = me_user * hist_count + lax.axis_index("hist")
    turn = jnp.reshape(me % (HEAD // SLOTS), (1,)).astype(jnp.int32)
    packed, normed, slot = make_queries(
        turn,
        block_list,
        cand_group.reshape(1, rows),
        cand_user.reshape(1, rows),
        cand_embed,
        in_gain,
        w_in,
        groups,
    )
    packed, keys, values, normed = lax.optimization_barrier(
        (packed, hist_keys, hist_values, normed)
    )
    arrived = lax.all_to_all(
        packed.reshape(devices, SLOTS + PAD, HEAD),
        everyone,
        split_axis=0,
        concat_axis=0,
        tiled=True,
    )
    kv = regroup(keys, values)
    gate, place = make_gate(slot, normed, w_in, groups * SLOTS)
    kv, arrived, gate, place = lax.optimization_barrier((kv, arrived, gate, place))
    kv = lax.all_to_all(kv, "hist", split_axis=0, concat_axis=0, tiled=True)

    tags = arrived[:, SLOTS, :].astype(jnp.int32).reshape(-1, HEAD // SLOTS, HEAD)
    tags = jnp.sum(tags, axis=1).reshape(devices * SLOTS // CHUNK, CHUNK)
    counts = jnp.sum(
        tags[:, None, :] == jnp.arange(USERS, dtype=jnp.int32)[None, :, None],
        axis=2,
        dtype=jnp.int32,
    )
    listed = lax.dynamic_slice(
        arrived, (me_user * hist_count, SLOTS + 1, 0), (hist_count, 1, blocks_here)
    )
    listed = listed.astype(jnp.int32).reshape(1, -1)
    order = jnp.arange(hist_count * blocks_here, dtype=jnp.int32)
    where = jnp.sum(jnp.where(listed == order[:, None], order[None, :], 0), axis=1)
    pick, query = sort_queries(counts, tags, arrived)

    attended = attend(counts, where, hist_len, query, pick, kv)
    returned = lax.all_to_all(
        attended.reshape(devices, SLOTS, HEAD), everyone, split_axis=0, concat_axis=0, tiled=True
    )
    return finish(
        returned.reshape(groups, HEADS, SLOTS, HEAD), place, cand_embed, gate, attn_gain, w_out
    )


def solution(mesh):
    split = P(("user", "hist"))
    in_specs = (split, split, split, P("user"), split, split, split, P(), P(), P(), P())
    return jax.shard_map(body, mesh=mesh, in_specs=in_specs, out_specs=split, check_vma=False)
```

```python
import functools

import jax
import jax.numpy as jnp
from jax import lax
from jax.experimental import pallas as pl
from jax.experimental.pallas import tpu as pltpu
from jax.sharding import PartitionSpec as P

HEADS = 8
HEAD = 128
BLK = 128
BLK_USR = 16
USERS = 4
SLOTS = 32
CHUNK = 512
NOTE = 8
PAD = 16
SORTED = CHUNK + 128
COPY = 64
TILE = 256
KEYS = 1024
REST = 512
VMEM = 48 * 1024 * 1024

BF16 = jnp.bfloat16
F32 = jnp.float32


def dot(a, b, contract):
    return lax.dot_general(a, b, ((contract[0], contract[1]), ((), ())), preferred_element_type=F32)


def params():
    return pltpu.CompilerParams(vmem_limit_bytes=VMEM)


def vmem():
    return pl.BlockSpec(memory_space=pltpu.VMEM)


def smem():
    return pl.BlockSpec(memory_space=pltpu.SMEM)


def regroup_kernel(keys_ref, values_ref, out_ref):
    out_ref[0, :, :HEAD] = keys_ref[...]
    out_ref[0, :, HEAD:] = values_ref[...]


def regroup(keys, values):
    rows = keys.shape[0]
    return pl.pallas_call(
        regroup_kernel,
        grid=(HEADS,),
        out_shape=jax.ShapeDtypeStruct((HEADS, rows, 2 * HEAD), BF16),
        in_specs=[pl.BlockSpec((rows, HEAD), lambda h: (0, h))] * 2,
        out_specs=pl.BlockSpec((1, rows, 2 * HEAD), lambda h: (h, 0, 0)),
        compiler_params=params(),
        name="regroup",
    )(keys, values)


def query_kernel(
    turn_ref,
    list_hbm,
    group_hbm,
    user_hbm,
    embed_hbm,
    gain_hbm,
    w_hbm,
    packed_hbm,
    normed_ref,
    slot_ref,
    listed,
    group_ref,
    user_ref,
    embed_ref,
    gain_ref,
    w_ref,
    packed_ref,
    sems,
    w_sems,
    out_sems,
):
    rows = embed_ref.shape[0]
    groups = packed_hbm.shape[0]
    slots = groups * SLOTS
    steps, _, step = w_ref.shape
    fetches = [
        pltpu.make_async_copy(source, target, sems.at[i])
        for i, (source, target) in enumerate(
            (
                (group_hbm, group_ref),
                (user_hbm, user_ref),
                (embed_hbm, embed_ref),
                (gain_hbm, gain_ref),
                (list_hbm, listed),
            )
        )
    ]
    for fetch in fetches:
        fetch.start()
    blocks = [
        pltpu.make_async_copy(w_hbm.at[:, pl.ds(i * step, step)], w_ref.at[i], w_sems.at[i])
        for i in range(steps)
    ]
    for block in blocks:
        block.start()

    fetches[0].wait()
    group = group_ref[...]
    member = (group == lax.broadcasted_iota(jnp.int32, (groups, rows), 0)).astype(F32)
    before = (
        lax.broadcasted_iota(jnp.int32, (rows, rows), 0)
        < lax.broadcasted_iota(jnp.int32, (rows, rows), 1)
    ).astype(BF16)
    count = dot(member.astype(BF16), before, ((1,), (0,)))
    position = jnp.sum(count * member, axis=0, keepdims=True).astype(jnp.int32)
    slot = group * SLOTS + position
    slot_ref[...] = slot
    place = (slot == lax.broadcasted_iota(jnp.int32, (slots, rows), 0)).astype(BF16)
    fetches[1].wait()
    offset = turn_ref[0] * SLOTS
    lanes = lax.broadcasted_iota(jnp.int32, (HEAD, rows), 0) == position + offset
    users = member * (user_ref[...] - USERS).astype(F32)
    tags = dot(users.astype(BF16), lanes.astype(BF16), ((1,), (1,)))
    own = lax.broadcasted_iota(jnp.int32, tags.shape, 1) - offset
    tags = tags + jnp.where((own >= 0) & (own < SLOTS), USERS, 0).astype(F32)
    fetches[4].wait()
    lane = lax.broadcasted_iota(jnp.int32, (groups, NOTE, HEAD), 2)
    row = lax.broadcasted_iota(jnp.int32, (groups, NOTE, HEAD), 1)
    blocks_here = jnp.zeros((groups, NOTE, HEAD), jnp.int32)
    for b in range(list_hbm.shape[1]):
        blocks_here = jnp.where(lane == b, listed[0, b], blocks_here)
    tags = jnp.broadcast_to(tags.reshape(groups, 1, HEAD), (groups, NOTE, HEAD))
    notes = jnp.where(
        row == 0, tags, jnp.where(row == 1, blocks_here.astype(F32), 0.0)
    ).astype(BF16)

    fetches[2].wait()
    fetches[3].wait()
    values = embed_ref[...].astype(F32)
    scaling = lax.rsqrt(jnp.mean(values * values, axis=-1, keepdims=True) + 1e-06)
    normed = (values * scaling * gain_ref[...]).astype(BF16)
    normed_ref[...] = normed
    stores = []
    for i in range(steps):
        blocks[i].wait()
        query = dot(normed, w_ref[i], ((1,), (0,)))
        query = (query / (1.0 + jnp.exp(-query))).astype(BF16)
        packed = dot(place, query, ((1,), (0,))).astype(BF16)
        for j in range(step // HEAD):
            h = i * (step // HEAD) + j
            packed_ref[h, :, :SLOTS] = packed[:, j * HEAD : (j + 1) * HEAD].reshape(
                groups, SLOTS, HEAD
            )
            packed_ref[h, :, SLOTS:] = notes
            store = pltpu.make_async_copy(packed_ref.at[h], packed_hbm.at[:, h], out_sems.at[h])
            store.start()
            stores.append(store)
    for store in stores:
        store.wait()


def make_queries(turn, listed, group, user, embed, gain, w_in, groups):
    rows, width = embed.shape
    step = 2 * HEAD
    hbm = pl.BlockSpec(memory_space=pltpu.HBM)
    return pl.pallas_call(
        query_kernel,
        out_shape=(
            jax.ShapeDtypeStruct((groups, HEADS, SLOTS + NOTE, HEAD), BF16),
            jax.ShapeDtypeStruct((rows, width), BF16),
            jax.ShapeDtypeStruct((1, rows), jnp.int32),
        ),
        in_specs=[smem()] + [hbm] * 6,
        out_specs=(hbm, vmem(), vmem()),
        scratch_shapes=[
            pltpu.SMEM(listed.shape, jnp.int32),
            pltpu.VMEM((1, rows), jnp.int32),
            pltpu.VMEM((1, rows), jnp.int32),
            pltpu.VMEM((rows, width), BF16),
            pltpu.VMEM((1, width), F32),
            pltpu.VMEM((width // step, width, step), BF16),
            pltpu.VMEM((HEADS, groups, SLOTS + NOTE, HEAD), BF16),
            pltpu.SemaphoreType.DMA((5,)),
            pltpu.SemaphoreType.DMA((width // step,)),
            pltpu.SemaphoreType.DMA((HEADS,)),
        ],
        compiler_params=pltpu.CompilerParams(vmem_limit_bytes=64 * 1024 * 1024),
        name="make_queries",
    )(turn, listed, group, user, embed, gain.reshape(1, width), w_in)


def gate_kernel(slot_ref, normed_ref, w_ref, gate_ref, place_ref):
    rows = normed_ref.shape[0]
    gate = dot(normed_ref[...], w_ref[...], ((1,), (0,)))
    gate_ref[...] = (gate / (1.0 + jnp.exp(-gate))).astype(BF16)
    column = jnp.broadcast_to(slot_ref[...].astype(F32), (8, rows)).T[:, :1].astype(jnp.int32)
    lane = lax.broadcasted_iota(jnp.int32, place_ref.shape, 1)
    place_ref[...] = (column == lane).astype(BF16)


def make_gate(slot, normed, w_in, slots):
    rows, width = normed.shape
    return pl.pallas_call(
        gate_kernel,
        grid=(1,),
        out_shape=(
            jax.ShapeDtypeStruct((rows, width), BF16),
            jax.ShapeDtypeStruct((rows, slots), BF16),
        ),
        in_specs=[
            pl.BlockSpec((1, rows), lambda i: (0, 0)),
            pl.BlockSpec((rows, width), lambda i: (0, 0)),
            pl.BlockSpec((width, width), lambda i: (0, 1)),
        ],
        out_specs=(
            pl.BlockSpec((rows, width), lambda i: (0, 0)),
            pl.BlockSpec((rows, slots), lambda i: (0, 0)),
        ),
        compiler_params=params(),
        name="make_gate",
    )(slot, normed, w_in)


def padded(count):
    return (count + (PAD - 1)) // PAD * PAD


def bases(counts_ref, chunks):
    starts, sizes, start = [], [], jnp.int32(0)
    for u in range(USERS):
        size = jnp.int32(0)
        for c in range(chunks):
            size = size + padded(counts_ref[c, u])
        starts.append(start)
        sizes.append(size)
        start = start + size
    return starts, sizes


def copy_rows(count, source, start, target, end):
    def step(i, carry):
        rows = source[pl.ds(pl.multiple_of(start + i * COPY, PAD), COPY), :]
        target[pl.ds(pl.multiple_of(end + i * COPY, PAD), COPY), :] = rows
        return carry

    lax.fori_loop(0, (count + (COPY - 1)) // COPY, step, 0)


def runs(counts_ref, c):
    starts, start = [], jnp.int32(0)
    for u in range(USERS):
        starts.append(start)
        start = start + padded(counts_ref[c, u])
    return starts


def sort_kernel(counts_ref, tags_ref, query_ref, pick_ref, sorted_ref, chunk_ref):
    chunks = tags_ref.shape[0]
    sources = CHUNK // SLOTS
    earlier = (
        lax.broadcasted_iota(jnp.int32, (CHUNK, CHUNK), 0)
        < lax.broadcasted_iota(jnp.int32, (CHUNK, CHUNK), 1)
    ).astype(BF16)
    places = []
    for c in range(chunks):
        tags = tags_ref[c : c + 1, :]
        lanes = (tags == lax.broadcasted_iota(jnp.int32, (8, CHUNK), 0)).astype(F32)
        rank = dot(lanes.astype(BF16), earlier, ((1,), (0,))).astype(jnp.int32)
        starts = runs(counts_ref, c)
        place = jnp.full((1, CHUNK), -1, jnp.int32)
        for u in range(USERS):
            place = jnp.where(tags == u, rank[u : u + 1, :] + starts[u], place)
        places.append(place)
        pick = (lax.broadcasted_iota(jnp.int32, (SORTED, CHUNK), 0) == place).astype(BF16)
        query = query_ref[c * sources : (c + 1) * sources, :SLOTS].reshape(CHUNK, HEAD)
        chunk_ref[c * SORTED : (c + 1) * SORTED, :] = dot(pick, query, ((1,), (0,))).astype(BF16)
    chunk_ref[chunks * SORTED :, :] = jnp.zeros((COPY, HEAD), BF16)
    sorted_ref[...] = jnp.zeros_like(sorted_ref)
    row = jnp.int32(0)
    for u in range(USERS):
        for c in range(chunks):
            count = counts_ref[c, u]
            copy_rows(count, chunk_ref, c * SORTED + runs(counts_ref, c)[u], sorted_ref, row)
            row = row + padded(count)
    columns = jnp.concatenate(places, axis=0).astype(F32).T.astype(jnp.int32)
    for c in range(chunks):
        lane = lax.broadcasted_iota(jnp.int32, (CHUNK, SORTED), 1)
        pick_ref[c] = (columns[:, c : c + 1] == lane).astype(BF16)


def sort_queries(counts, tags, query):
    chunks = tags.shape[0]
    return pl.pallas_call(
        sort_kernel,
        out_shape=(
            jax.ShapeDtypeStruct((chunks, CHUNK, SORTED), BF16),
            jax.ShapeDtypeStruct((chunks * SORTED + TILE, HEAD), BF16),
        ),
        in_specs=[smem(), vmem(), vmem()],
        out_specs=(vmem(), vmem()),
        scratch_shapes=[pltpu.VMEM((chunks * SORTED + COPY, HEAD), BF16)],
        compiler_params=params(),
        name="sort_queries",
    )(counts, tags, query)


def attend_kernel(
    counts_ref,
    where_ref,
    length_ref,
    query_ref,
    pick_hbm,
    kv_hbm,
    out_ref,
    kv,
    pick,
    total,
    chunk,
    kv_sem,
    pick_sem,
):
    chunks = out_ref.shape[0]
    blocks = kv_hbm.shape[1] // BLK
    starts, sizes = bases(counts_ref, chunks)
    fetch = pltpu.make_async_copy(kv_hbm, kv, kv_sem)
    fetch.start()
    picks = pltpu.make_async_copy(pick_hbm, pick, pick_sem)
    picks.start()
    total[...] = jnp.zeros_like(total)
    chunk[...] = jnp.zeros_like(chunk)
    fetch.wait()

    scale = 0.5 * HEAD ** (-0.5)

    def partial(query, u, first, count, limit):
        parts = []
        for j in range(count):
            at = where_ref[u * BLK_USR + first + j]
            row = pl.multiple_of(at % blocks * BLK, BLK)
            parts.append(kv[at // blocks, pl.ds(row, BLK), :])
        part = jnp.concatenate(parts, axis=0)
        half = dot(query, part[:, :HEAD], ((1,), (1,))) * scale
        weight = half + half * jnp.tanh(half)
        if limit is not None:
            column = lax.broadcasted_iota(jnp.int32, weight.shape, 1)
            weight = jnp.where(column < limit, weight, 0.0)
        return dot(weight.astype(BF16), part[:, HEAD:], ((1,), (0,)))

    for u in range(USERS):
        length = length_ref[u]
        whole = length // KEYS
        rest = (length - whole * KEYS + (REST - 1)) // REST

        def tile(i, carry, u=u, length=length, whole=whole, rest=rest):
            at = pl.multiple_of(starts[u] + i * TILE, PAD)
            query = query_ref[pl.ds(at, TILE), :]

            def step(k, running):
                return running + partial(query, u, k * (KEYS // BLK), KEYS // BLK, None)

            def end(k, running):
                first = whole * KEYS + k * REST
                return running + partial(query, u, first // BLK, REST // BLK, length - first)

            running = lax.fori_loop(0, whole, step, jnp.zeros((TILE, HEAD), F32))
            running = lax.fori_loop(0, rest, end, running)
            total[pl.ds(at, TILE), :] = running.astype(BF16)
            return carry

        lax.fori_loop(0, (sizes[u] + (TILE - 1)) // TILE, tile, 0)

    picks.wait()
    rows = list(starts)
    for c in range(chunks):
        run = runs(counts_ref, c)
        for u in range(USERS):
            count = counts_ref[c, u]
            copy_rows(count, total, rows[u], chunk, c * SORTED + run[u])
            rows[u] = rows[u] + padded(count)
    for c in range(chunks):
        out_ref[c] = dot(pick[c], chunk[c * SORTED : (c + 1) * SORTED, :], ((1,), (0,))).astype(BF16)


def attend(counts, where, length, query, pick, kv):
    chunks = pick.shape[0]
    rows = query.shape[0]
    anywhere = pl.BlockSpec(memory_space=pl.ANY)
    return pl.pallas_call(
        attend_kernel,
        out_shape=jax.ShapeDtypeStruct((chunks, CHUNK, HEAD), BF16),
        in_specs=[smem(), smem(), smem(), vmem(), anywhere, anywhere],
        out_specs=vmem(),
        scratch_shapes=[
            pltpu.VMEM(kv.shape, BF16),
            pltpu.VMEM(pick.shape, BF16),
            pltpu.VMEM((rows, HEAD), BF16),
            pltpu.VMEM((chunks * SORTED + COPY, HEAD), BF16),
            pltpu.SemaphoreType.DMA,
            pltpu.SemaphoreType.DMA,
        ],
        compiler_params=params(),
        name="attend",
    )(counts, where, length, query, pick, kv)


def finish_kernel(returned_ref, place_ref, embed_ref, gate_ref, gain_ref, w_ref, out_ref, attended):
    slots = place_ref.shape[1]
    for h in range(HEADS):
        attended[:, h * HEAD : (h + 1) * HEAD] = dot(
            place_ref[...], returned_ref[:, h].reshape(slots, HEAD), ((1,), (0,))
        )
    picked = attended[...]
    scaling = lax.rsqrt(jnp.mean(picked * picked, axis=-1, keepdims=True) + 1e-05)
    gated = (picked * scaling * gain_ref[...] * gate_ref[...].astype(F32)).astype(BF16)
    mixed = embed_ref[...].astype(F32) + dot(gated, w_ref[...], ((1,), (0,)))
    out_ref[...] = mixed.astype(BF16)


def finish(returned, place, embed, gate, gain, w_out):
    rows, width = embed.shape
    return pl.pallas_call(
        finish_kernel,
        out_shape=jax.ShapeDtypeStruct((rows, width), BF16),
        in_specs=[vmem()] * 6,
        out_specs=vmem(),
        scratch_shapes=[pltpu.VMEM((rows, width), F32)],
        compiler_params=params(),
        name="finish",
    )(returned, place, embed, gate, gain.reshape(1, width), w_out)


def body(
    cand_embed,
    cand_group,
    cand_user,
    hist_len,
    block_list,
    hist_keys,
    hist_values,
    in_gain,
    w_in,
    attn_gain,
    w_out,
):
    groups = lax.axis_size("user")
    hist_count = lax.axis_size("hist")
    devices = groups * hist_count
    everyone = ("user", "hist")
    blocks_here = block_list.shape[0]

    rows = cand_embed.shape[0]
    me_user = lax.axis_index("user")
    me = me_user * hist_count + lax.axis_index("hist")
    turn = jnp.reshape(me % (HEAD // SLOTS), (1,)).astype(jnp.int32)
    packed, normed, slot = make_queries(
        turn,
        block_list.reshape(1, -1),
        cand_group.reshape(1, rows),
        cand_user.reshape(1, rows),
        cand_embed,
        in_gain,
        w_in,
        groups,
    )
    packed, keys, values, normed = lax.optimization_barrier(
        (packed, hist_keys, hist_values, normed)
    )
    arrived = lax.all_to_all(
        packed.reshape(devices, SLOTS + NOTE, HEAD),
        everyone,
        split_axis=0,
        concat_axis=0,
        tiled=True,
    )
    kv = regroup(keys, values)
    gate, place = make_gate(slot, normed, w_in, groups * SLOTS)
    kv, arrived, gate, place = lax.optimization_barrier((kv, arrived, gate, place))
    kv = lax.all_to_all(kv, "hist", split_axis=0, concat_axis=0, tiled=True)

    tags = arrived[:, SLOTS, :].astype(jnp.int32).reshape(-1, HEAD // SLOTS, HEAD)
    tags = jnp.sum(tags, axis=1).reshape(devices * SLOTS // CHUNK, CHUNK)
    counts = jnp.sum(
        tags[:, None, :] == jnp.arange(USERS, dtype=jnp.int32)[None, :, None],
        axis=2,
        dtype=jnp.int32,
    )
    listed = lax.dynamic_slice(
        arrived, (me_user * hist_count, SLOTS + 1, 0), (hist_count, 1, blocks_here)
    )
    listed = listed.astype(jnp.int32).reshape(1, -1)
    order = jnp.arange(hist_count * blocks_here, dtype=jnp.int32)
    where = jnp.sum(jnp.where(listed == order[:, None], order[None, :], 0), axis=1)
    pick, query = sort_queries(counts, tags, arrived)

    attended = attend(counts, where, hist_len, query, pick, kv)
    returned = lax.all_to_all(
        attended.reshape(devices, SLOTS, HEAD), everyone, split_axis=0, concat_axis=0, tiled=True
    )
    return finish(
        returned.reshape(groups, HEADS, SLOTS, HEAD), place, cand_embed, gate, attn_gain, w_out
    )


def solution(mesh):
    split = P(("user", "hist"))
    in_specs = (split, split, split, P("user"), split, split, split, P(), P(), P(), P())
    return jax.shard_map(body, mesh=mesh, in_specs=in_specs, out_specs=split, check_vma=False)
```

```python
import functools

import jax
import jax.numpy as jnp
from jax import lax
from jax.experimental import pallas as pl
from jax.experimental.pallas import tpu as pltpu
from jax.sharding import PartitionSpec as P

HEADS = 8
HEAD = 128
BLK = 128
BLK_USR = 16
USERS = 4
SLOTS = 32
CHUNK = 512
NOTE = 8
PAD = 16
SORTED = CHUNK + 128
COPY = 64
TILES = (256, 384, 512, 640, 768)
TILE = TILES[-1]
KEYS = 1024
REST = 512
VMEM = 48 * 1024 * 1024

BF16 = jnp.bfloat16
F32 = jnp.float32


def dot(a, b, contract):
    return lax.dot_general(a, b, ((contract[0], contract[1]), ((), ())), preferred_element_type=F32)


def params():
    return pltpu.CompilerParams(vmem_limit_bytes=VMEM)


def vmem():
    return pl.BlockSpec(memory_space=pltpu.VMEM)


def smem():
    return pl.BlockSpec(memory_space=pltpu.SMEM)


def regroup_kernel(keys_ref, values_ref, out_ref):
    out_ref[0, :, :HEAD] = keys_ref[...]
    out_ref[0, :, HEAD:] = values_ref[...]


def regroup(keys, values):
    rows = keys.shape[0]
    return pl.pallas_call(
        regroup_kernel,
        grid=(HEADS,),
        out_shape=jax.ShapeDtypeStruct((HEADS, rows, 2 * HEAD), BF16),
        in_specs=[pl.BlockSpec((rows, HEAD), lambda h: (0, h))] * 2,
        out_specs=pl.BlockSpec((1, rows, 2 * HEAD), lambda h: (h, 0, 0)),
        compiler_params=params(),
        name="regroup",
    )(keys, values)


def query_kernel(
    turn_ref,
    list_hbm,
    group_hbm,
    user_hbm,
    embed_hbm,
    gain_hbm,
    w_hbm,
    packed_hbm,
    normed_ref,
    slot_ref,
    listed,
    group_ref,
    user_ref,
    embed_ref,
    gain_ref,
    w_ref,
    packed_ref,
    sems,
    w_sems,
    out_sems,
):
    rows = embed_ref.shape[0]
    groups = packed_hbm.shape[0]
    slots = groups * SLOTS
    steps, _, step = w_ref.shape
    fetches = [
        pltpu.make_async_copy(source, target, sems.at[i])
        for i, (source, target) in enumerate(
            (
                (group_hbm, group_ref),
                (user_hbm, user_ref),
                (embed_hbm, embed_ref),
                (gain_hbm, gain_ref),
                (list_hbm, listed),
            )
        )
    ]
    for fetch in fetches:
        fetch.start()
    blocks = [
        pltpu.make_async_copy(w_hbm.at[:, pl.ds(i * step, step)], w_ref.at[i], w_sems.at[i])
        for i in range(steps)
    ]
    for block in blocks:
        block.start()

    fetches[0].wait()
    group = group_ref[...]
    member = (group == lax.broadcasted_iota(jnp.int32, (groups, rows), 0)).astype(F32)
    before = (
        lax.broadcasted_iota(jnp.int32, (rows, rows), 0)
        < lax.broadcasted_iota(jnp.int32, (rows, rows), 1)
    ).astype(BF16)
    count = dot(member.astype(BF16), before, ((1,), (0,)))
    position = jnp.sum(count * member, axis=0, keepdims=True).astype(jnp.int32)
    slot = group * SLOTS + position
    slot_ref[...] = slot
    place = (slot == lax.broadcasted_iota(jnp.int32, (slots, rows), 0)).astype(BF16)
    fetches[1].wait()
    offset = turn_ref[0] * SLOTS
    lanes = lax.broadcasted_iota(jnp.int32, (HEAD, rows), 0) == position + offset
    users = member * (user_ref[...] - USERS).astype(F32)
    tags = dot(users.astype(BF16), lanes.astype(BF16), ((1,), (1,)))
    own = lax.broadcasted_iota(jnp.int32, tags.shape, 1) - offset
    tags = tags + jnp.where((own >= 0) & (own < SLOTS), USERS, 0).astype(F32)
    fetches[4].wait()
    lane = lax.broadcasted_iota(jnp.int32, (groups, NOTE, HEAD), 2)
    row = lax.broadcasted_iota(jnp.int32, (groups, NOTE, HEAD), 1)
    blocks_here = jnp.zeros((groups, NOTE, HEAD), jnp.int32)
    for b in range(list_hbm.shape[1]):
        blocks_here = jnp.where(lane == b, listed[0, b], blocks_here)
    tags = jnp.broadcast_to(tags.reshape(groups, 1, HEAD), (groups, NOTE, HEAD))
    notes = jnp.where(
        row == 0, tags, jnp.where(row == 1, blocks_here.astype(F32), 0.0)
    ).astype(BF16)

    fetches[2].wait()
    fetches[3].wait()
    values = embed_ref[...].astype(F32)
    scaling = lax.rsqrt(jnp.mean(values * values, axis=-1, keepdims=True) + 1e-06)
    normed = (values * scaling * gain_ref[...]).astype(BF16)
    normed_ref[...] = normed
    stores = []
    for i in range(steps):
        blocks[i].wait()
        query = dot(normed, w_ref[i], ((1,), (0,)))
        query = (query / (1.0 + jnp.exp(-query))).astype(BF16)
        packed = dot(place, query, ((1,), (0,))).astype(BF16)
        for j in range(step // HEAD):
            h = i * (step // HEAD) + j
            packed_ref[h, :, :SLOTS] = packed[:, j * HEAD : (j + 1) * HEAD].reshape(
                groups, SLOTS, HEAD
            )
            packed_ref[h, :, SLOTS:] = notes
            store = pltpu.make_async_copy(packed_ref.at[h], packed_hbm.at[:, h], out_sems.at[h])
            store.start()
            stores.append(store)
    for store in stores:
        store.wait()


def make_queries(turn, listed, group, user, embed, gain, w_in, groups):
    rows, width = embed.shape
    step = 2 * HEAD
    hbm = pl.BlockSpec(memory_space=pltpu.HBM)
    return pl.pallas_call(
        query_kernel,
        out_shape=(
            jax.ShapeDtypeStruct((groups, HEADS, SLOTS + NOTE, HEAD), BF16),
            jax.ShapeDtypeStruct((rows, width), BF16),
            jax.ShapeDtypeStruct((1, rows), jnp.int32),
        ),
        in_specs=[smem()] + [hbm] * 6,
        out_specs=(hbm, vmem(), vmem()),
        scratch_shapes=[
            pltpu.SMEM(listed.shape, jnp.int32),
            pltpu.VMEM((1, rows), jnp.int32),
            pltpu.VMEM((1, rows), jnp.int32),
            pltpu.VMEM((rows, width), BF16),
            pltpu.VMEM((1, width), F32),
            pltpu.VMEM((width // step, width, step), BF16),
            pltpu.VMEM((HEADS, groups, SLOTS + NOTE, HEAD), BF16),
            pltpu.SemaphoreType.DMA((5,)),
            pltpu.SemaphoreType.DMA((width // step,)),
            pltpu.SemaphoreType.DMA((HEADS,)),
        ],
        compiler_params=pltpu.CompilerParams(vmem_limit_bytes=64 * 1024 * 1024),
        name="make_queries",
    )(turn, listed, group, user, embed, gain.reshape(1, width), w_in)


def gate_kernel(slot_ref, normed_ref, w_ref, gate_ref, place_ref):
    rows = normed_ref.shape[0]
    gate = dot(normed_ref[...], w_ref[...], ((1,), (0,)))
    gate_ref[...] = (gate / (1.0 + jnp.exp(-gate))).astype(BF16)
    column = jnp.broadcast_to(slot_ref[...].astype(F32), (8, rows)).T[:, :1].astype(jnp.int32)
    lane = lax.broadcasted_iota(jnp.int32, place_ref.shape, 1)
    place_ref[...] = (column == lane).astype(BF16)


def make_gate(slot, normed, w_in, slots):
    rows, width = normed.shape
    return pl.pallas_call(
        gate_kernel,
        grid=(1,),
        out_shape=(
            jax.ShapeDtypeStruct((rows, width), BF16),
            jax.ShapeDtypeStruct((rows, slots), BF16),
        ),
        in_specs=[
            pl.BlockSpec((1, rows), lambda i: (0, 0)),
            pl.BlockSpec((rows, width), lambda i: (0, 0)),
            pl.BlockSpec((width, width), lambda i: (0, 1)),
        ],
        out_specs=(
            pl.BlockSpec((rows, width), lambda i: (0, 0)),
            pl.BlockSpec((rows, slots), lambda i: (0, 0)),
        ),
        compiler_params=params(),
        name="make_gate",
    )(slot, normed, w_in)


def padded(count):
    return (count + (PAD - 1)) // PAD * PAD


def bases(counts_ref, chunks):
    starts, sizes, start = [], [], jnp.int32(0)
    for u in range(USERS):
        size = jnp.int32(0)
        for c in range(chunks):
            size = size + padded(counts_ref[c, u])
        starts.append(start)
        sizes.append(size)
        start = start + size
    return starts, sizes


def copy_rows(count, source, start, target, end):
    def step(i, carry):
        rows = source[pl.ds(pl.multiple_of(start + i * COPY, PAD), COPY), :]
        target[pl.ds(pl.multiple_of(end + i * COPY, PAD), COPY), :] = rows
        return carry

    lax.fori_loop(0, (count + (COPY - 1)) // COPY, step, 0)


def runs(counts_ref, c):
    starts, start = [], jnp.int32(0)
    for u in range(USERS):
        starts.append(start)
        start = start + padded(counts_ref[c, u])
    return starts


def sort_kernel(counts_ref, tags_ref, query_ref, pick_ref, sorted_ref, chunk_ref):
    chunks = tags_ref.shape[0]
    sources = CHUNK // SLOTS
    earlier = (
        lax.broadcasted_iota(jnp.int32, (CHUNK, CHUNK), 0)
        < lax.broadcasted_iota(jnp.int32, (CHUNK, CHUNK), 1)
    ).astype(BF16)
    places = []
    for c in range(chunks):
        tags = tags_ref[c : c + 1, :]
        lanes = (tags == lax.broadcasted_iota(jnp.int32, (8, CHUNK), 0)).astype(F32)
        rank = dot(lanes.astype(BF16), earlier, ((1,), (0,))).astype(jnp.int32)
        starts = runs(counts_ref, c)
        place = jnp.full((1, CHUNK), -1, jnp.int32)
        for u in range(USERS):
            place = jnp.where(tags == u, rank[u : u + 1, :] + starts[u], place)
        places.append(place)
        pick = (lax.broadcasted_iota(jnp.int32, (SORTED, CHUNK), 0) == place).astype(BF16)
        query = query_ref[c * sources : (c + 1) * sources, :SLOTS].reshape(CHUNK, HEAD)
        chunk_ref[c * SORTED : (c + 1) * SORTED, :] = dot(pick, query, ((1,), (0,))).astype(BF16)
    chunk_ref[chunks * SORTED :, :] = jnp.zeros((COPY, HEAD), BF16)
    sorted_ref[...] = jnp.zeros_like(sorted_ref)
    row = jnp.int32(0)
    for u in range(USERS):
        for c in range(chunks):
            count = counts_ref[c, u]
            copy_rows(count, chunk_ref, c * SORTED + runs(counts_ref, c)[u], sorted_ref, row)
            row = row + padded(count)
    columns = jnp.concatenate(places, axis=0).astype(F32).T.astype(jnp.int32)
    for c in range(chunks):
        lane = lax.broadcasted_iota(jnp.int32, (CHUNK, SORTED), 1)
        pick_ref[c] = (columns[:, c : c + 1] == lane).astype(BF16)


def sort_queries(counts, tags, query):
    chunks = tags.shape[0]
    return pl.pallas_call(
        sort_kernel,
        out_shape=(
            jax.ShapeDtypeStruct((chunks, CHUNK, SORTED), BF16),
            jax.ShapeDtypeStruct((chunks * SORTED + TILE, HEAD), BF16),
        ),
        in_specs=[smem(), vmem(), vmem()],
        out_specs=(vmem(), vmem()),
        scratch_shapes=[pltpu.VMEM((chunks * SORTED + COPY, HEAD), BF16)],
        compiler_params=params(),
        name="sort_queries",
    )(counts, tags, query)


def attend_kernel(
    counts_ref,
    where_ref,
    length_ref,
    query_ref,
    pick_hbm,
    kv_hbm,
    out_ref,
    kv,
    pick,
    total,
    chunk,
    start_ref,
    size_ref,
    kv_sem,
    pick_sem,
):
    chunks = out_ref.shape[0]
    blocks = kv_hbm.shape[1] // BLK
    starts, sizes = bases(counts_ref, chunks)
    fetch = pltpu.make_async_copy(kv_hbm, kv, kv_sem)
    fetch.start()
    total[...] = jnp.zeros_like(total)
    chunk[...] = jnp.zeros_like(chunk)
    fetch.wait()
    picks = pltpu.make_async_copy(pick_hbm, pick, pick_sem)
    picks.start()

    scale = 0.5 * HEAD ** (-0.5)

    def partial(query, u, first, count, limit):
        parts = []
        for j in range(count):
            at = where_ref[u * BLK_USR + first + j]
            row = pl.multiple_of(at % blocks * BLK, BLK)
            parts.append(kv[at // blocks, pl.ds(row, BLK), :])
        part = jnp.concatenate(parts, axis=0)
        half = dot(query, part[:, :HEAD], ((1,), (1,))) * scale
        weight = half + half * jnp.tanh(half)
        if limit is not None:
            column = lax.broadcasted_iota(jnp.int32, weight.shape, 1)
            weight = jnp.where(column < limit, weight, 0.0)
        return dot(weight.astype(BF16), part[:, HEAD:], ((1,), (0,)))

    def attend_tile(size, u, at):
        length = length_ref[u]
        whole = length // KEYS
        rest = (length - whole * KEYS + (REST - 1)) // REST
        query = query_ref[pl.ds(at, size), :]

        def step(k, running):
            return running + partial(query, u, k * (KEYS // BLK), KEYS // BLK, None)

        def end(k, running):
            first = whole * KEYS + k * REST
            return running + partial(query, u, first // BLK, REST // BLK, length - first)

        running = lax.fori_loop(0, whole, step, jnp.zeros((size, HEAD), F32))
        running = lax.fori_loop(0, rest, end, running)
        total[pl.ds(at, size), :] = running.astype(BF16)

    for u in range(USERS):
        start_ref[u] = starts[u]
        size_ref[u] = sizes[u]

    def attend_user(u, carry):
        def attend_rows(state):
            at, left = state
            for shorter, size in zip((0,) + TILES[:-1], TILES):
                fits = left > shorter
                if size < TILE:
                    fits = fits & (left <= size)

                @pl.when(fits)
                def _(size=size):
                    attend_tile(size, u, pl.multiple_of(at, PAD))

            return at + TILE, left - TILE

        lax.while_loop(lambda state: state[1] > 0, attend_rows, (start_ref[u], size_ref[u]))
        return carry

    lax.fori_loop(0, USERS, attend_user, 0)

    picks.wait()
    rows = list(starts)
    for c in range(chunks):
        run = runs(counts_ref, c)
        for u in range(USERS):
            count = counts_ref[c, u]
            copy_rows(count, total, rows[u], chunk, c * SORTED + run[u])
            rows[u] = rows[u] + padded(count)
    for c in range(chunks):
        used = runs(counts_ref, c)[USERS - 1] + counts_ref[c, USERS - 1]
        for shorter, size in ((0, 256), (256, 512), (512, SORTED)):

            @pl.when((used > shorter) & (used <= size) if shorter else used <= size)
            def _(c=c, size=size):
                rows = chunk[c * SORTED : c * SORTED + size, :]
                out_ref[c] = dot(pick[c, :, :size], rows, ((1,), (0,))).astype(BF16)


def attend(counts, where, length, query, pick, kv):
    chunks = pick.shape[0]
    rows = query.shape[0]
    anywhere = pl.BlockSpec(memory_space=pl.ANY)
    return pl.pallas_call(
        attend_kernel,
        out_shape=jax.ShapeDtypeStruct((chunks, CHUNK, HEAD), BF16),
        in_specs=[smem(), smem(), smem(), vmem(), anywhere, anywhere],
        out_specs=vmem(),
        scratch_shapes=[
            pltpu.VMEM(kv.shape, BF16),
            pltpu.VMEM(pick.shape, BF16),
            pltpu.VMEM((rows, HEAD), BF16),
            pltpu.VMEM((chunks * SORTED + COPY, HEAD), BF16),
            pltpu.SMEM((USERS,), jnp.int32),
            pltpu.SMEM((USERS,), jnp.int32),
            pltpu.SemaphoreType.DMA,
            pltpu.SemaphoreType.DMA,
        ],
        compiler_params=params(),
        name="attend",
    )(counts, where, length, query, pick, kv)


def finish_kernel(returned_ref, place_ref, embed_ref, gate_ref, gain_ref, w_ref, out_ref, attended):
    slots = place_ref.shape[1]
    for h in range(HEADS):
        attended[:, h * HEAD : (h + 1) * HEAD] = dot(
            place_ref[...], returned_ref[:, h].reshape(slots, HEAD), ((1,), (0,))
        )
    picked = attended[...]
    scaling = lax.rsqrt(jnp.mean(picked * picked, axis=-1, keepdims=True) + 1e-05)
    gated = (picked * scaling * gain_ref[...] * gate_ref[...].astype(F32)).astype(BF16)
    mixed = embed_ref[...].astype(F32) + dot(gated, w_ref[...], ((1,), (0,)))
    out_ref[...] = mixed.astype(BF16)


def finish(returned, place, embed, gate, gain, w_out):
    rows, width = embed.shape
    return pl.pallas_call(
        finish_kernel,
        out_shape=jax.ShapeDtypeStruct((rows, width), BF16),
        in_specs=[vmem()] * 6,
        out_specs=vmem(),
        scratch_shapes=[pltpu.VMEM((rows, width), F32)],
        compiler_params=params(),
        name="finish",
    )(returned, place, embed, gate, gain.reshape(1, width), w_out)


def body(
    cand_embed,
    cand_group,
    cand_user,
    hist_len,
    block_list,
    hist_keys,
    hist_values,
    in_gain,
    w_in,
    attn_gain,
    w_out,
):
    groups = lax.axis_size("user")
    hist_count = lax.axis_size("hist")
    devices = groups * hist_count
    everyone = ("user", "hist")
    blocks_here = block_list.shape[0]

    rows = cand_embed.shape[0]
    me_user = lax.axis_index("user")
    me = me_user * hist_count + lax.axis_index("hist")
    turn = jnp.reshape(me % (HEAD // SLOTS), (1,)).astype(jnp.int32)
    packed, normed, slot = make_queries(
        turn,
        block_list.reshape(1, -1),
        cand_group.reshape(1, rows),
        cand_user.reshape(1, rows),
        cand_embed,
        in_gain,
        w_in,
        groups,
    )
    packed, keys, values, normed = lax.optimization_barrier(
        (packed, hist_keys, hist_values, normed)
    )
    arrived = lax.all_to_all(
        packed.reshape(devices, SLOTS + NOTE, HEAD),
        everyone,
        split_axis=0,
        concat_axis=0,
        tiled=True,
    )
    kv = regroup(keys, values)
    gate, place = make_gate(slot, normed, w_in, groups * SLOTS)
    kv, arrived, gate, place = lax.optimization_barrier((kv, arrived, gate, place))
    kv = lax.all_to_all(kv, "hist", split_axis=0, concat_axis=0, tiled=True)

    tags = arrived[:, SLOTS, :].astype(jnp.int32).reshape(-1, HEAD // SLOTS, HEAD)
    tags = jnp.sum(tags, axis=1).reshape(devices * SLOTS // CHUNK, CHUNK)
    counts = jnp.sum(
        tags[:, None, :] == jnp.arange(USERS, dtype=jnp.int32)[None, :, None],
        axis=2,
        dtype=jnp.int32,
    )
    listed = lax.dynamic_slice(
        arrived, (me_user * hist_count, SLOTS + 1, 0), (hist_count, 1, blocks_here)
    )
    listed = listed.astype(jnp.int32).reshape(1, -1)
    order = jnp.arange(hist_count * blocks_here, dtype=jnp.int32)
    where = jnp.sum(jnp.where(listed == order[:, None], order[None, :], 0), axis=1)
    pick, query = sort_queries(counts, tags, arrived)

    attended = attend(counts, where, hist_len, query, pick, kv)
    returned = lax.all_to_all(
        attended.reshape(devices, SLOTS, HEAD), everyone, split_axis=0, concat_axis=0, tiled=True
    )
    return finish(
        returned.reshape(groups, HEADS, SLOTS, HEAD), place, cand_embed, gate, attn_gain, w_out
    )


def solution(mesh):
    split = P(("user", "hist"))
    in_specs = (split, split, split, P("user"), split, split, split, P(), P(), P(), P())
    return jax.shard_map(body, mesh=mesh, in_specs=in_specs, out_specs=split, check_vma=False)
```

```python
import functools

import jax
import jax.numpy as jnp
from jax import lax
from jax.experimental import pallas as pl
from jax.experimental.pallas import tpu as pltpu
from jax.sharding import PartitionSpec as P

HEADS = 8
HEAD = 128
BLK = 128
BLK_USR = 16
USERS = 4
SLOTS = 32
CHUNK = 512
NOTE = 8
PAD = 16
SORTED = CHUNK + 128
COPY = 64
SHORT = 160
TILES = (256, 384, 512, 576, 640, 704, 768)
TILE = TILES[-1]
KEYS = 1024
UNIT = 256
VMEM = 48 * 1024 * 1024

BF16 = jnp.bfloat16
F32 = jnp.float32


def dot(a, b, contract):
    return lax.dot_general(a, b, ((contract[0], contract[1]), ((), ())), preferred_element_type=F32)


def silu(value):
    half = 0.5 * value
    return half + half * jnp.tanh(half)


def params():
    return pltpu.CompilerParams(vmem_limit_bytes=VMEM)


def vmem():
    return pl.BlockSpec(memory_space=pltpu.VMEM)


def smem():
    return pl.BlockSpec(memory_space=pltpu.SMEM)


def regroup_kernel(keys_ref, values_ref, out_ref):
    out_ref[0, :, :HEAD] = keys_ref[...]
    out_ref[0, :, HEAD:] = values_ref[...]


def regroup(keys, values):
    rows = keys.shape[0]
    return pl.pallas_call(
        regroup_kernel,
        grid=(HEADS,),
        out_shape=jax.ShapeDtypeStruct((HEADS, rows, 2 * HEAD), BF16),
        in_specs=[pl.BlockSpec((rows, HEAD), lambda h: (0, h))] * 2,
        out_specs=pl.BlockSpec((1, rows, 2 * HEAD), lambda h: (h, 0, 0)),
        compiler_params=params(),
        name="regroup",
    )(keys, values)


def query_kernel(
    turn_ref,
    list_hbm,
    group_hbm,
    user_hbm,
    embed_hbm,
    gain_hbm,
    w_hbm,
    packed_hbm,
    normed_ref,
    slot_ref,
    listed,
    group_ref,
    user_ref,
    embed_ref,
    gain_ref,
    w_ref,
    packed_ref,
    sems,
    w_sems,
    out_sems,
):
    rows = embed_ref.shape[0]
    groups = packed_hbm.shape[0]
    slots = groups * SLOTS
    steps, _, step = w_ref.shape
    fetches = [
        pltpu.make_async_copy(source, target, sems.at[i])
        for i, (source, target) in enumerate(
            (
                (group_hbm, group_ref),
                (user_hbm, user_ref),
                (embed_hbm, embed_ref),
                (gain_hbm, gain_ref),
                (list_hbm, listed),
            )
        )
    ]
    for fetch in fetches:
        fetch.start()
    blocks = [
        pltpu.make_async_copy(w_hbm.at[:, pl.ds(i * step, step)], w_ref.at[i], w_sems.at[i])
        for i in range(steps)
    ]
    for block in blocks:
        block.start()

    fetches[0].wait()
    group = group_ref[...]
    member = (group == lax.broadcasted_iota(jnp.int32, (groups, rows), 0)).astype(F32)
    before = (
        lax.broadcasted_iota(jnp.int32, (rows, rows), 0)
        < lax.broadcasted_iota(jnp.int32, (rows, rows), 1)
    ).astype(BF16)
    count = dot(member.astype(BF16), before, ((1,), (0,)))
    position = jnp.sum(count * member, axis=0, keepdims=True).astype(jnp.int32)
    slot = group * SLOTS + position
    slot_ref[...] = slot
    place = (slot == lax.broadcasted_iota(jnp.int32, (slots, rows), 0)).astype(BF16)
    fetches[1].wait()
    offset = turn_ref[0] * SLOTS
    lanes = lax.broadcasted_iota(jnp.int32, (HEAD, rows), 0) == position + offset
    users = member * (user_ref[...] - USERS).astype(F32)
    tags = dot(users.astype(BF16), lanes.astype(BF16), ((1,), (1,)))
    own = lax.broadcasted_iota(jnp.int32, tags.shape, 1) - offset
    tags = tags + jnp.where((own >= 0) & (own < SLOTS), USERS, 0).astype(F32)
    fetches[4].wait()
    lane = lax.broadcasted_iota(jnp.int32, (groups, NOTE, HEAD), 2)
    row = lax.broadcasted_iota(jnp.int32, (groups, NOTE, HEAD), 1)
    blocks_here = jnp.zeros((groups, NOTE, HEAD), jnp.int32)
    for b in range(list_hbm.shape[1]):
        blocks_here = jnp.where(lane == b, listed[0, b], blocks_here)
    tags = jnp.broadcast_to(tags.reshape(groups, 1, HEAD), (groups, NOTE, HEAD))
    notes = jnp.where(
        row == 0, tags, jnp.where(row == 1, blocks_here.astype(F32), 0.0)
    ).astype(BF16)

    fetches[2].wait()
    fetches[3].wait()
    values = embed_ref[...].astype(F32)
    scaling = lax.rsqrt(jnp.mean(values * values, axis=-1, keepdims=True) + 1e-06)
    normed = (values * scaling * gain_ref[...]).astype(BF16)
    normed_ref[...] = normed
    stores = []
    for i in range(steps):
        blocks[i].wait()
        query = dot(normed, w_ref[i], ((1,), (0,)))
        query = silu(query).astype(BF16)
        packed = dot(place, query, ((1,), (0,))).astype(BF16)
        for j in range(step // HEAD):
            h = i * (step // HEAD) + j
            packed_ref[h, :, :SLOTS] = packed[:, j * HEAD : (j + 1) * HEAD].reshape(
                groups, SLOTS, HEAD
            )
            packed_ref[h, :, SLOTS:] = notes
            store = pltpu.make_async_copy(packed_ref.at[h], packed_hbm.at[:, h], out_sems.at[h])
            store.start()
            stores.append(store)
    for store in stores:
        store.wait()


def make_queries(turn, listed, group, user, embed, gain, w_in, groups):
    rows, width = embed.shape
    step = 2 * HEAD
    hbm = pl.BlockSpec(memory_space=pltpu.HBM)
    return pl.pallas_call(
        query_kernel,
        out_shape=(
            jax.ShapeDtypeStruct((groups, HEADS, SLOTS + NOTE, HEAD), BF16),
            jax.ShapeDtypeStruct((rows, width), BF16),
            jax.ShapeDtypeStruct((1, rows), jnp.int32),
        ),
        in_specs=[smem()] + [hbm] * 6,
        out_specs=(hbm, vmem(), vmem()),
        scratch_shapes=[
            pltpu.SMEM(listed.shape, jnp.int32),
            pltpu.VMEM((1, rows), jnp.int32),
            pltpu.VMEM((1, rows), jnp.int32),
            pltpu.VMEM((rows, width), BF16),
            pltpu.VMEM((1, width), F32),
            pltpu.VMEM((width // step, width, step), BF16),
            pltpu.VMEM((HEADS, groups, SLOTS + NOTE, HEAD), BF16),
            pltpu.SemaphoreType.DMA((5,)),
            pltpu.SemaphoreType.DMA((width // step,)),
            pltpu.SemaphoreType.DMA((HEADS,)),
        ],
        compiler_params=pltpu.CompilerParams(vmem_limit_bytes=64 * 1024 * 1024),
        name="make_queries",
    )(turn, listed, group, user, embed, gain.reshape(1, width), w_in)


def gate_kernel(slot_ref, normed_ref, w_ref, gate_ref, place_ref):
    rows = normed_ref.shape[0]
    gate = dot(normed_ref[...], w_ref[...], ((1,), (0,)))
    gate_ref[...] = silu(gate).astype(BF16)
    column = jnp.broadcast_to(slot_ref[...].astype(F32), (8, rows)).T[:, :1].astype(jnp.int32)
    lane = lax.broadcasted_iota(jnp.int32, place_ref.shape, 1)
    place_ref[...] = (column == lane).astype(BF16)


def make_gate(slot, normed, w_in, slots):
    rows, width = normed.shape
    return pl.pallas_call(
        gate_kernel,
        grid=(1,),
        out_shape=(
            jax.ShapeDtypeStruct((rows, width), BF16),
            jax.ShapeDtypeStruct((rows, slots), BF16),
        ),
        in_specs=[
            pl.BlockSpec((1, rows), lambda i: (0, 0)),
            pl.BlockSpec((rows, width), lambda i: (0, 0)),
            pl.BlockSpec((width, width), lambda i: (0, 1)),
        ],
        out_specs=(
            pl.BlockSpec((rows, width), lambda i: (0, 0)),
            pl.BlockSpec((rows, slots), lambda i: (0, 0)),
        ),
        compiler_params=params(),
        name="make_gate",
    )(slot, normed, w_in)


def padded(count):
    return (count + (PAD - 1)) // PAD * PAD


def bases(counts_ref, chunks):
    starts, sizes, start = [], [], jnp.int32(0)
    for u in range(USERS):
        size = jnp.int32(0)
        for c in range(chunks):
            size = size + padded(counts_ref[c, u])
        starts.append(start)
        sizes.append(size)
        start = start + size
    return starts, sizes


def copy_rows(count, source, start, target, end):
    def step(i, carry):
        rows = source[pl.ds(pl.multiple_of(start + i * COPY, PAD), COPY), :]
        target[pl.ds(pl.multiple_of(end + i * COPY, PAD), COPY), :] = rows
        return carry

    lax.fori_loop(0, (count + (COPY - 1)) // COPY, step, 0)


def runs(counts_ref, c):
    starts, start = [], jnp.int32(0)
    for u in range(USERS):
        starts.append(start)
        start = start + padded(counts_ref[c, u])
    return starts


def sort_kernel(counts_ref, tags_ref, query_ref, pick_ref, sorted_ref, chunk_ref):
    chunks = tags_ref.shape[0]
    sources = CHUNK // SLOTS
    earlier = (
        lax.broadcasted_iota(jnp.int32, (CHUNK, CHUNK), 0)
        < lax.broadcasted_iota(jnp.int32, (CHUNK, CHUNK), 1)
    ).astype(BF16)
    places = []
    for c in range(chunks):
        tags = tags_ref[c : c + 1, :]
        lanes = (tags == lax.broadcasted_iota(jnp.int32, (8, CHUNK), 0)).astype(F32)
        rank = dot(lanes.astype(BF16), earlier, ((1,), (0,))).astype(jnp.int32)
        starts = runs(counts_ref, c)
        place = jnp.full((1, CHUNK), -1, jnp.int32)
        for u in range(USERS):
            place = jnp.where(tags == u, rank[u : u + 1, :] + starts[u], place)
        places.append(place)
        pick = (lax.broadcasted_iota(jnp.int32, (SORTED, CHUNK), 0) == place).astype(BF16)
        query = query_ref[c * sources : (c + 1) * sources, :SLOTS].reshape(CHUNK, HEAD)
        chunk_ref[c * SORTED : (c + 1) * SORTED, :] = dot(pick, query, ((1,), (0,))).astype(BF16)
    chunk_ref[chunks * SORTED :, :] = jnp.zeros((COPY, HEAD), BF16)
    sorted_ref[...] = jnp.zeros_like(sorted_ref)
    row = jnp.int32(0)
    for u in range(USERS):
        for c in range(chunks):
            count = counts_ref[c, u]
            copy_rows(count, chunk_ref, c * SORTED + runs(counts_ref, c)[u], sorted_ref, row)
            row = row + padded(count)
    columns = jnp.concatenate(places, axis=0).astype(F32).T.astype(jnp.int32)
    for c in range(chunks):
        lane = lax.broadcasted_iota(jnp.int32, (CHUNK, SORTED), 1)
        pick_ref[c] = (columns[:, c : c + 1] == lane).astype(BF16)


def sort_queries(counts, tags, query):
    chunks = tags.shape[0]
    return pl.pallas_call(
        sort_kernel,
        out_shape=(
            jax.ShapeDtypeStruct((chunks, CHUNK, SORTED), BF16),
            jax.ShapeDtypeStruct((chunks * SORTED + TILE, HEAD), BF16),
        ),
        in_specs=[smem(), vmem(), vmem()],
        out_specs=(vmem(), vmem()),
        scratch_shapes=[pltpu.VMEM((chunks * SORTED + COPY, HEAD), BF16)],
        compiler_params=params(),
        name="sort_queries",
    )(counts, tags, query)


def attend_kernel(
    counts_ref,
    where_ref,
    length_ref,
    query_ref,
    pick_hbm,
    kv_hbm,
    out_ref,
    kv,
    pick,
    total,
    start_ref,
    size_ref,
    kv_sem,
    pick_sem,
    *chunk,
):
    chunks = out_ref.shape[0]
    blocks = kv_hbm.shape[1] // BLK
    starts, sizes = bases(counts_ref, chunks)
    fetch = pltpu.make_async_copy(kv_hbm, kv, kv_sem)
    fetch.start()
    total[...] = jnp.zeros_like(total)
    for part in chunk:
        part[...] = jnp.zeros_like(part)
    fetch.wait()
    picks = pltpu.make_async_copy(pick_hbm, pick, pick_sem)
    picks.start()

    scale = 0.5 * HEAD ** (-0.5)

    def partial(query, u, first, count, limit):
        parts = []
        for j in range(count):
            at = where_ref[u * BLK_USR + first + j]
            row = pl.multiple_of(at % blocks * BLK, BLK)
            parts.append(kv[at // blocks, pl.ds(row, BLK), :])
        part = jnp.concatenate(parts, axis=0)
        half = dot(query, part[:, :HEAD], ((1,), (1,))) * scale
        weight = half + half * jnp.tanh(half)
        if limit is not None:
            column = lax.broadcasted_iota(jnp.int32, weight.shape, 1)
            weight = jnp.where(column < limit, weight, 0.0)
        return dot(weight.astype(BF16), part[:, HEAD:], ((1,), (0,)))

    def attend_tile(size, u, at):
        length = length_ref[u]
        units = (length + (UNIT - 1)) // UNIT
        whole = (units - 1) // (KEYS // UNIT)
        query = query_ref[pl.ds(at, size), :]

        def step(k, running):
            return running + partial(query, u, k * (KEYS // BLK), KEYS // BLK, None)

        running = lax.fori_loop(0, whole, step, jnp.zeros((size, HEAD), F32))
        first = whole * KEYS
        for count in range(1, KEYS // UNIT + 1):

            @pl.when(units - whole * (KEYS // UNIT) == count)
            def _(count=count):
                rest = partial(query, u, first // BLK, count * UNIT // BLK, length - first)
                total[pl.ds(at, size), :] = (running + rest).astype(BF16)

    for u in range(USERS):
        start_ref[u] = starts[u]
        size_ref[u] = sizes[u]

    def attend_user(u, carry):
        def attend_rows(state):
            at, left = state
            for shorter, size in zip((0,) + TILES[:-1], TILES):
                fits = left > shorter
                if size < TILE:
                    fits = fits & (left <= size)

                @pl.when(fits)
                def _(size=size):
                    attend_tile(size, u, pl.multiple_of(at, PAD))

            return at + TILE, left - TILE

        lax.while_loop(lambda state: state[1] > 0, attend_rows, (start_ref[u], size_ref[u]))
        return carry

    lax.fori_loop(0, USERS, attend_user, 0)

    picks.wait()
    rows = list(starts)
    moves = []
    short = True
    for c in range(chunks):
        run = runs(counts_ref, c)
        for u in range(USERS):
            count = counts_ref[c, u]
            moves.append((c, count, rows[u], run[u]))
            rows[u] = rows[u] + padded(count)
            short = short & (count <= SHORT)
        short = short & (run[USERS - 1] + padded(counts_ref[c, USERS - 1]) <= CHUNK)

    def put_back(size):
        for c in range(chunks):
            out_ref[c] = dot(pick[c, :, :size], chunk[c][:size, :], ((1,), (0,))).astype(BF16)

    @pl.when(short)
    def _():
        for c, _, source, target in moves:
            run = total[pl.ds(pl.multiple_of(source, PAD), SHORT), :]
            chunk[c][pl.ds(pl.multiple_of(target, PAD), SHORT), :] = run
        put_back(CHUNK)

    @pl.when(jnp.logical_not(short))
    def _():
        for c, count, source, target in moves:
            copy_rows(count, total, source, chunk[c], target)
        put_back(SORTED)


def attend(counts, where, length, query, pick, kv):
    chunks = pick.shape[0]
    rows = query.shape[0]
    anywhere = pl.BlockSpec(memory_space=pl.ANY)
    return pl.pallas_call(
        attend_kernel,
        out_shape=jax.ShapeDtypeStruct((chunks, CHUNK, HEAD), BF16),
        in_specs=[smem(), smem(), smem(), vmem(), anywhere, anywhere],
        out_specs=vmem(),
        scratch_shapes=[
            pltpu.VMEM(kv.shape, BF16),
            pltpu.VMEM(pick.shape, BF16),
            pltpu.VMEM((rows, HEAD), BF16),
            pltpu.SMEM((USERS,), jnp.int32),
            pltpu.SMEM((USERS,), jnp.int32),
            pltpu.SemaphoreType.DMA,
            pltpu.SemaphoreType.DMA,
        ]
        + [pltpu.VMEM((SORTED + SHORT, HEAD), BF16)] * chunks,
        compiler_params=params(),
        name="attend",
    )(counts, where, length, query, pick, kv)


def finish_kernel(returned_ref, place_ref, embed_ref, gate_ref, gain_ref, w_ref, out_ref, attended):
    slots = place_ref.shape[1]
    for h in range(HEADS):
        attended[:, h * HEAD : (h + 1) * HEAD] = dot(
            place_ref[...], returned_ref[:, h].reshape(slots, HEAD), ((1,), (0,))
        )
    picked = attended[...]
    scaling = lax.rsqrt(jnp.mean(picked * picked, axis=-1, keepdims=True) + 1e-05)
    gated = (picked * scaling * gain_ref[...] * gate_ref[...].astype(F32)).astype(BF16)
    mixed = embed_ref[...].astype(F32) + dot(gated, w_ref[...], ((1,), (0,)))
    out_ref[...] = mixed.astype(BF16)


def finish(returned, place, embed, gate, gain, w_out):
    rows, width = embed.shape
    return pl.pallas_call(
        finish_kernel,
        out_shape=jax.ShapeDtypeStruct((rows, width), BF16),
        in_specs=[vmem()] * 6,
        out_specs=vmem(),
        scratch_shapes=[pltpu.VMEM((rows, width), F32)],
        compiler_params=params(),
        name="finish",
    )(returned, place, embed, gate, gain.reshape(1, width), w_out)


def body(
    cand_embed,
    cand_group,
    cand_user,
    hist_len,
    block_list,
    hist_keys,
    hist_values,
    in_gain,
    w_in,
    attn_gain,
    w_out,
):
    groups = lax.axis_size("user")
    hist_count = lax.axis_size("hist")
    devices = groups * hist_count
    everyone = ("user", "hist")
    blocks_here = block_list.shape[0]

    rows = cand_embed.shape[0]
    me_user = lax.axis_index("user")
    me = me_user * hist_count + lax.axis_index("hist")
    turn = jnp.reshape(me % (HEAD // SLOTS), (1,)).astype(jnp.int32)
    packed, normed, slot = make_queries(
        turn,
        block_list.reshape(1, -1),
        cand_group.reshape(1, rows),
        cand_user.reshape(1, rows),
        cand_embed,
        in_gain,
        w_in,
        groups,
    )
    packed, keys, values, normed = lax.optimization_barrier(
        (packed, hist_keys, hist_values, normed)
    )
    arrived = lax.all_to_all(
        packed.reshape(devices, SLOTS + NOTE, HEAD),
        everyone,
        split_axis=0,
        concat_axis=0,
        tiled=True,
    )
    kv = regroup(keys, values)
    gate, place = make_gate(slot, normed, w_in, groups * SLOTS)
    kv, arrived, gate, place = lax.optimization_barrier((kv, arrived, gate, place))
    kv = lax.all_to_all(kv, "hist", split_axis=0, concat_axis=0, tiled=True)

    tags = arrived[:, SLOTS, :].astype(jnp.int32).reshape(-1, HEAD // SLOTS, HEAD)
    tags = jnp.sum(tags, axis=1).reshape(devices * SLOTS // CHUNK, CHUNK)
    counts = jnp.sum(
        tags[:, None, :] == jnp.arange(USERS, dtype=jnp.int32)[None, :, None],
        axis=2,
        dtype=jnp.int32,
    )
    listed = lax.dynamic_slice(
        arrived, (me_user * hist_count, SLOTS + 1, 0), (hist_count, 1, blocks_here)
    )
    listed = listed.astype(jnp.int32).reshape(1, -1)
    order = jnp.arange(hist_count * blocks_here, dtype=jnp.int32)
    where = jnp.sum(jnp.where(listed == order[:, None], order[None, :], 0), axis=1)
    pick, query = sort_queries(counts, tags, arrived)

    attended = attend(counts, where, hist_len, query, pick, kv)
    returned = lax.all_to_all(
        attended.reshape(devices, SLOTS, HEAD), everyone, split_axis=0, concat_axis=0, tiled=True
    )
    return finish(
        returned.reshape(groups, HEADS, SLOTS, HEAD), place, cand_embed, gate, attn_gain, w_out
    )


def solution(mesh):
    split = P(("user", "hist"))
    in_specs = (split, split, split, P("user"), split, split, split, P(), P(), P(), P())
    return jax.shard_map(body, mesh=mesh, in_specs=in_specs, out_specs=split, check_vma=False)
```

```python
import functools

import jax
import jax.numpy as jnp
from jax import lax
from jax.experimental import pallas as pl
from jax.experimental.pallas import tpu as pltpu
from jax.sharding import PartitionSpec as P

HEADS = 8
HEAD = 128
BLK = 128
BLK_USR = 16
USERS = 4
SLOTS = 32
CHUNK = 512
NOTE = 8
PAD = 16
SORTED = CHUNK + 128
COPY = 64
SHORT = 160
TILES = (256, 512, 768)
TILE = TILES[-1]
KEYS = 1024
UNIT = 512
VMEM = 48 * 1024 * 1024

BF16 = jnp.bfloat16
F32 = jnp.float32


def dot(a, b, contract):
    return lax.dot_general(a, b, ((contract[0], contract[1]), ((), ())), preferred_element_type=F32)


def silu(value):
    half = 0.5 * value
    return half + half * jnp.tanh(half)


def params():
    return pltpu.CompilerParams(vmem_limit_bytes=VMEM)


def vmem():
    return pl.BlockSpec(memory_space=pltpu.VMEM)


def smem():
    return pl.BlockSpec(memory_space=pltpu.SMEM)


def regroup_kernel(keys_ref, values_ref, out_ref):
    out_ref[0, :, :HEAD] = keys_ref[...]
    out_ref[0, :, HEAD:] = values_ref[...]


def regroup(keys, values):
    rows = keys.shape[0]
    return pl.pallas_call(
        regroup_kernel,
        grid=(HEADS,),
        out_shape=jax.ShapeDtypeStruct((HEADS, rows, 2 * HEAD), BF16),
        in_specs=[pl.BlockSpec((rows, HEAD), lambda h: (0, h))] * 2,
        out_specs=pl.BlockSpec((1, rows, 2 * HEAD), lambda h: (h, 0, 0)),
        compiler_params=params(),
        name="regroup",
    )(keys, values)


def query_kernel(
    turn_ref,
    list_hbm,
    group_hbm,
    user_hbm,
    embed_hbm,
    gain_hbm,
    w_hbm,
    packed_hbm,
    normed_ref,
    slot_ref,
    listed,
    group_ref,
    user_ref,
    embed_ref,
    gain_ref,
    w_ref,
    packed_ref,
    sems,
    w_sems,
    out_sems,
):
    rows = embed_ref.shape[0]
    groups = packed_hbm.shape[0]
    slots = groups * SLOTS
    steps, _, step = w_ref.shape
    fetches = [
        pltpu.make_async_copy(source, target, sems.at[i])
        for i, (source, target) in enumerate(
            (
                (group_hbm, group_ref),
                (user_hbm, user_ref),
                (embed_hbm, embed_ref),
                (gain_hbm, gain_ref),
                (list_hbm, listed),
            )
        )
    ]
    for fetch in fetches:
        fetch.start()
    blocks = [
        pltpu.make_async_copy(w_hbm.at[:, pl.ds(i * step, step)], w_ref.at[i], w_sems.at[i])
        for i in range(steps)
    ]
    for block in blocks:
        block.start()

    fetches[0].wait()
    group = group_ref[...]
    member = (group == lax.broadcasted_iota(jnp.int32, (groups, rows), 0)).astype(F32)
    before = (
        lax.broadcasted_iota(jnp.int32, (rows, rows), 0)
        < lax.broadcasted_iota(jnp.int32, (rows, rows), 1)
    ).astype(BF16)
    count = dot(member.astype(BF16), before, ((1,), (0,)))
    position = jnp.sum(count * member, axis=0, keepdims=True).astype(jnp.int32)
    slot = group * SLOTS + position
    slot_ref[...] = slot
    place = (slot == lax.broadcasted_iota(jnp.int32, (slots, rows), 0)).astype(BF16)
    fetches[1].wait()
    offset = turn_ref[0] * SLOTS
    lanes = lax.broadcasted_iota(jnp.int32, (HEAD, rows), 0) == position + offset
    users = member * (user_ref[...] - USERS).astype(F32)
    tags = dot(users.astype(BF16), lanes.astype(BF16), ((1,), (1,)))
    own = lax.broadcasted_iota(jnp.int32, tags.shape, 1) - offset
    tags = tags + jnp.where((own >= 0) & (own < SLOTS), USERS, 0).astype(F32)
    fetches[4].wait()
    lane = lax.broadcasted_iota(jnp.int32, (groups, NOTE, HEAD), 2)
    row = lax.broadcasted_iota(jnp.int32, (groups, NOTE, HEAD), 1)
    blocks_here = jnp.zeros((groups, NOTE, HEAD), jnp.int32)
    for b in range(list_hbm.shape[1]):
        blocks_here = jnp.where(lane == b, listed[0, b], blocks_here)
    tags = jnp.broadcast_to(tags.reshape(groups, 1, HEAD), (groups, NOTE, HEAD))
    notes = jnp.where(
        row == 0, tags, jnp.where(row == 1, blocks_here.astype(F32), 0.0)
    ).astype(BF16)

    fetches[2].wait()
    fetches[3].wait()
    values = embed_ref[...].astype(F32)
    scaling = lax.rsqrt(jnp.mean(values * values, axis=-1, keepdims=True) + 1e-06)
    normed = (values * scaling * gain_ref[...]).astype(BF16)
    normed_ref[...] = normed
    stores = []
    for i in range(steps):
        blocks[i].wait()
        query = dot(normed, w_ref[i], ((1,), (0,)))
        query = silu(query).astype(BF16)
        packed = dot(place, query, ((1,), (0,))).astype(BF16)
        for j in range(step // HEAD):
            h = i * (step // HEAD) + j
            packed_ref[h, :, :SLOTS] = packed[:, j * HEAD : (j + 1) * HEAD].reshape(
                groups, SLOTS, HEAD
            )
            packed_ref[h, :, SLOTS:] = notes
            store = pltpu.make_async_copy(packed_ref.at[h], packed_hbm.at[:, h], out_sems.at[h])
            store.start()
            stores.append(store)
    for store in stores:
        store.wait()


def make_queries(turn, listed, group, user, embed, gain, w_in, groups):
    rows, width = embed.shape
    step = 2 * HEAD
    hbm = pl.BlockSpec(memory_space=pltpu.HBM)
    return pl.pallas_call(
        query_kernel,
        out_shape=(
            jax.ShapeDtypeStruct((groups, HEADS, SLOTS + NOTE, HEAD), BF16),
            jax.ShapeDtypeStruct((rows, width), BF16),
            jax.ShapeDtypeStruct((1, rows), jnp.int32),
        ),
        in_specs=[smem()] + [hbm] * 6,
        out_specs=(hbm, vmem(), vmem()),
        scratch_shapes=[
            pltpu.SMEM(listed.shape, jnp.int32),
            pltpu.VMEM((1, rows), jnp.int32),
            pltpu.VMEM((1, rows), jnp.int32),
            pltpu.VMEM((rows, width), BF16),
            pltpu.VMEM((1, width), F32),
            pltpu.VMEM((width // step, width, step), BF16),
            pltpu.VMEM((HEADS, groups, SLOTS + NOTE, HEAD), BF16),
            pltpu.SemaphoreType.DMA((5,)),
            pltpu.SemaphoreType.DMA((width // step,)),
            pltpu.SemaphoreType.DMA((HEADS,)),
        ],
        compiler_params=pltpu.CompilerParams(vmem_limit_bytes=64 * 1024 * 1024),
        name="make_queries",
    )(turn, listed, group, user, embed, gain.reshape(1, width), w_in)


def gate_kernel(slot_ref, normed_ref, w_ref, gate_ref, place_ref):
    rows = normed_ref.shape[0]
    gate = dot(normed_ref[...], w_ref[...], ((1,), (0,)))
    gate_ref[...] = silu(gate).astype(BF16)
    column = jnp.broadcast_to(slot_ref[...].astype(F32), (8, rows)).T[:, :1].astype(jnp.int32)
    lane = lax.broadcasted_iota(jnp.int32, place_ref.shape, 1)
    place_ref[...] = (column == lane).astype(BF16)


def make_gate(slot, normed, w_in, slots):
    rows, width = normed.shape
    return pl.pallas_call(
        gate_kernel,
        grid=(1,),
        out_shape=(
            jax.ShapeDtypeStruct((rows, width), BF16),
            jax.ShapeDtypeStruct((rows, slots), BF16),
        ),
        in_specs=[
            pl.BlockSpec((1, rows), lambda i: (0, 0)),
            pl.BlockSpec((rows, width), lambda i: (0, 0)),
            pl.BlockSpec((width, width), lambda i: (0, 1)),
        ],
        out_specs=(
            pl.BlockSpec((rows, width), lambda i: (0, 0)),
            pl.BlockSpec((rows, slots), lambda i: (0, 0)),
        ),
        compiler_params=params(),
        name="make_gate",
    )(slot, normed, w_in)


def padded(count):
    return (count + (PAD - 1)) // PAD * PAD


def bases(counts_ref, chunks):
    starts, sizes, start = [], [], jnp.int32(0)
    for u in range(USERS):
        size = jnp.int32(0)
        for c in range(chunks):
            size = size + padded(counts_ref[c, u])
        starts.append(start)
        sizes.append(size)
        start = start + size
    return starts, sizes


def copy_rows(count, source, start, target, end):
    def step(i, carry):
        rows = source[pl.ds(pl.multiple_of(start + i * COPY, PAD), COPY), :]
        target[pl.ds(pl.multiple_of(end + i * COPY, PAD), COPY), :] = rows
        return carry

    lax.fori_loop(0, (count + (COPY - 1)) // COPY, step, 0)


def runs(counts_ref, c):
    starts, start = [], jnp.int32(0)
    for u in range(USERS):
        starts.append(start)
        start = start + padded(counts_ref[c, u])
    return starts


def sort_kernel(counts_ref, tags_ref, query_ref, pick_ref, sorted_ref, chunk_ref):
    chunks = tags_ref.shape[0]
    sources = CHUNK // SLOTS
    earlier = (
        lax.broadcasted_iota(jnp.int32, (CHUNK, CHUNK), 0)
        < lax.broadcasted_iota(jnp.int32, (CHUNK, CHUNK), 1)
    ).astype(BF16)
    places = []
    for c in range(chunks):
        tags = tags_ref[c : c + 1, :]
        lanes = (tags == lax.broadcasted_iota(jnp.int32, (8, CHUNK), 0)).astype(F32)
        rank = dot(lanes.astype(BF16), earlier, ((1,), (0,))).astype(jnp.int32)
        starts = runs(counts_ref, c)
        place = jnp.full((1, CHUNK), -1, jnp.int32)
        for u in range(USERS):
            place = jnp.where(tags == u, rank[u : u + 1, :] + starts[u], place)
        places.append(place)
        pick = (lax.broadcasted_iota(jnp.int32, (SORTED, CHUNK), 0) == place).astype(BF16)
        query = query_ref[c * sources : (c + 1) * sources, :SLOTS].reshape(CHUNK, HEAD)
        chunk_ref[c * SORTED : (c + 1) * SORTED, :] = dot(pick, query, ((1,), (0,))).astype(BF16)
    chunk_ref[chunks * SORTED :, :] = jnp.zeros((COPY, HEAD), BF16)
    sorted_ref[...] = jnp.zeros_like(sorted_ref)
    row = jnp.int32(0)
    for u in range(USERS):
        for c in range(chunks):
            count = counts_ref[c, u]
            copy_rows(count, chunk_ref, c * SORTED + runs(counts_ref, c)[u], sorted_ref, row)
            row = row + padded(count)
    columns = jnp.concatenate(places, axis=0).astype(F32).T.astype(jnp.int32)
    for c in range(chunks):
        lane = lax.broadcasted_iota(jnp.int32, (CHUNK, SORTED), 1)
        pick_ref[c] = (columns[:, c : c + 1] == lane).astype(BF16)


def sort_queries(counts, tags, query):
    chunks = tags.shape[0]
    return pl.pallas_call(
        sort_kernel,
        out_shape=(
            jax.ShapeDtypeStruct((chunks, CHUNK, SORTED), BF16),
            jax.ShapeDtypeStruct((chunks * SORTED + TILE, HEAD), BF16),
        ),
        in_specs=[smem(), vmem(), vmem()],
        out_specs=(vmem(), vmem()),
        scratch_shapes=[pltpu.VMEM((chunks * SORTED + COPY, HEAD), BF16)],
        compiler_params=params(),
        name="sort_queries",
    )(counts, tags, query)


def attend_kernel(
    counts_ref,
    where_ref,
    length_ref,
    query_ref,
    pick_hbm,
    kv_hbm,
    out_ref,
    kv,
    pick,
    total,
    start_ref,
    size_ref,
    kv_sem,
    pick_sem,
    *chunk,
):
    chunks = out_ref.shape[0]
    blocks = kv_hbm.shape[1] // BLK
    starts, sizes = bases(counts_ref, chunks)
    fetch = pltpu.make_async_copy(kv_hbm, kv, kv_sem)
    fetch.start()
    total[...] = jnp.zeros_like(total)
    for part in chunk:
        part[...] = jnp.zeros_like(part)
    fetch.wait()
    picks = pltpu.make_async_copy(pick_hbm, pick, pick_sem)
    picks.start()

    scale = 0.5 * HEAD ** (-0.5)

    def partial(query, u, first, count, limit):
        parts = []
        for j in range(count):
            at = where_ref[u * BLK_USR + first + j]
            row = pl.multiple_of(at % blocks * BLK, BLK)
            parts.append(kv[at // blocks, pl.ds(row, BLK), :])
        part = jnp.concatenate(parts, axis=0)
        half = dot(query, part[:, :HEAD], ((1,), (1,))) * scale
        weight = half + half * jnp.tanh(half)
        if limit is not None:
            column = lax.broadcasted_iota(jnp.int32, weight.shape, 1)
            weight = jnp.where(column < limit, weight, 0.0)
        return dot(weight.astype(BF16), part[:, HEAD:], ((1,), (0,)))

    def attend_tile(size, u, at):
        length = length_ref[u]
        units = (length + (UNIT - 1)) // UNIT
        whole = (units - 1) // (KEYS // UNIT)
        query = query_ref[pl.ds(at, size), :]

        def step(k, running):
            return running + partial(query, u, k * (KEYS // BLK), KEYS // BLK, None)

        running = lax.fori_loop(0, whole, step, jnp.zeros((size, HEAD), F32))
        first = whole * KEYS
        for count in range(1, KEYS // UNIT + 1):

            @pl.when(units - whole * (KEYS // UNIT) == count)
            def _(count=count):
                rest = partial(query, u, first // BLK, count * UNIT // BLK, length - first)
                total[pl.ds(at, size), :] = (running + rest).astype(BF16)

    for u in range(USERS):
        start_ref[u] = starts[u]
        size_ref[u] = sizes[u]

    def attend_user(u, carry):
        def attend_rows(state):
            at, left = state
            for shorter, size in zip((0,) + TILES[:-1], TILES):
                fits = left > shorter
                if size < TILE:
                    fits = fits & (left <= size)

                @pl.when(fits)
                def _(size=size):
                    attend_tile(size, u, pl.multiple_of(at, PAD))

            return at + TILE, left - TILE

        lax.while_loop(lambda state: state[1] > 0, attend_rows, (start_ref[u], size_ref[u]))
        return carry

    lax.fori_loop(0, USERS, attend_user, 0)

    picks.wait()
    rows = list(starts)
    moves = []
    short = True
    for c in range(chunks):
        run = runs(counts_ref, c)
        for u in range(USERS):
            count = counts_ref[c, u]
            moves.append((c, count, rows[u], run[u]))
            rows[u] = rows[u] + padded(count)
            short = short & (count <= SHORT)
        short = short & (run[USERS - 1] + padded(counts_ref[c, USERS - 1]) <= CHUNK)

    def put_back(size):
        for c in range(chunks):
            out_ref[c] = dot(pick[c, :, :size], chunk[c][:size, :], ((1,), (0,))).astype(BF16)

    @pl.when(short)
    def _():
        for c, _, source, target in moves:
            run = total[pl.ds(pl.multiple_of(source, PAD), SHORT), :]
            chunk[c][pl.ds(pl.multiple_of(target, PAD), SHORT), :] = run
        put_back(CHUNK)

    @pl.when(jnp.logical_not(short))
    def _():
        for c, count, source, target in moves:
            copy_rows(count, total, source, chunk[c], target)
        put_back(SORTED)


def attend(counts, where, length, query, pick, kv):
    chunks = pick.shape[0]
    rows = query.shape[0]
    anywhere = pl.BlockSpec(memory_space=pl.ANY)
    return pl.pallas_call(
        attend_kernel,
        out_shape=jax.ShapeDtypeStruct((chunks, CHUNK, HEAD), BF16),
        in_specs=[smem(), smem(), smem(), vmem(), anywhere, anywhere],
        out_specs=vmem(),
        scratch_shapes=[
            pltpu.VMEM(kv.shape, BF16),
            pltpu.VMEM(pick.shape, BF16),
            pltpu.VMEM((rows, HEAD), BF16),
            pltpu.SMEM((USERS,), jnp.int32),
            pltpu.SMEM((USERS,), jnp.int32),
            pltpu.SemaphoreType.DMA,
            pltpu.SemaphoreType.DMA,
        ]
        + [pltpu.VMEM((SORTED + SHORT, HEAD), BF16)] * chunks,
        compiler_params=params(),
        name="attend",
    )(counts, where, length, query, pick, kv)


def finish_kernel(returned_ref, place_ref, embed_ref, gate_ref, gain_ref, w_ref, out_ref, attended):
    slots = place_ref.shape[1]
    for h in range(HEADS):
        attended[:, h * HEAD : (h + 1) * HEAD] = dot(
            place_ref[...], returned_ref[:, h].reshape(slots, HEAD), ((1,), (0,))
        )
    picked = attended[...]
    scaling = lax.rsqrt(jnp.mean(picked * picked, axis=-1, keepdims=True) + 1e-05)
    gated = (picked * scaling * gain_ref[...] * gate_ref[...].astype(F32)).astype(BF16)
    mixed = embed_ref[...].astype(F32) + dot(gated, w_ref[...], ((1,), (0,)))
    out_ref[...] = mixed.astype(BF16)


def finish(returned, place, embed, gate, gain, w_out):
    rows, width = embed.shape
    return pl.pallas_call(
        finish_kernel,
        out_shape=jax.ShapeDtypeStruct((rows, width), BF16),
        in_specs=[vmem()] * 6,
        out_specs=vmem(),
        scratch_shapes=[pltpu.VMEM((rows, width), F32)],
        compiler_params=params(),
        name="finish",
    )(returned, place, embed, gate, gain.reshape(1, width), w_out)


def body(
    cand_embed,
    cand_group,
    cand_user,
    hist_len,
    block_list,
    hist_keys,
    hist_values,
    in_gain,
    w_in,
    attn_gain,
    w_out,
):
    groups = lax.axis_size("user")
    hist_count = lax.axis_size("hist")
    devices = groups * hist_count
    everyone = ("user", "hist")
    blocks_here = block_list.shape[0]

    rows = cand_embed.shape[0]
    me_user = lax.axis_index("user")
    me = me_user * hist_count + lax.axis_index("hist")
    turn = jnp.reshape(me % (HEAD // SLOTS), (1,)).astype(jnp.int32)
    packed, normed, slot = make_queries(
        turn,
        block_list.reshape(1, -1),
        cand_group.reshape(1, rows),
        cand_user.reshape(1, rows),
        cand_embed,
        in_gain,
        w_in,
        groups,
    )
    packed, keys, values, normed = lax.optimization_barrier(
        (packed, hist_keys, hist_values, normed)
    )
    arrived = lax.all_to_all(
        packed.reshape(devices, SLOTS + NOTE, HEAD),
        everyone,
        split_axis=0,
        concat_axis=0,
        tiled=True,
    )
    kv = regroup(keys, values)
    gate, place = make_gate(slot, normed, w_in, groups * SLOTS)
    kv, arrived, gate, place = lax.optimization_barrier((kv, arrived, gate, place))
    kv = lax.all_to_all(kv, "hist", split_axis=0, concat_axis=0, tiled=True)

    tags = arrived[:, SLOTS, :].astype(jnp.int32).reshape(-1, HEAD // SLOTS, HEAD)
    tags = jnp.sum(tags, axis=1).reshape(devices * SLOTS // CHUNK, CHUNK)
    counts = jnp.sum(
        tags[:, None, :] == jnp.arange(USERS, dtype=jnp.int32)[None, :, None],
        axis=2,
        dtype=jnp.int32,
    )
    listed = lax.dynamic_slice(
        arrived, (me_user * hist_count, SLOTS + 1, 0), (hist_count, 1, blocks_here)
    )
    listed = listed.astype(jnp.int32).reshape(1, -1)
    order = jnp.arange(hist_count * blocks_here, dtype=jnp.int32)
    where = jnp.sum(jnp.where(listed == order[:, None], order[None, :], 0), axis=1)
    pick, query = sort_queries(counts, tags, arrived)

    attended = attend(counts, where, hist_len, query, pick, kv)
    returned = lax.all_to_all(
        attended.reshape(devices, SLOTS, HEAD), everyone, split_axis=0, concat_axis=0, tiled=True
    )
    return finish(
        returned.reshape(groups, HEADS, SLOTS, HEAD), place, cand_embed, gate, attn_gain, w_out
    )


def solution(mesh):
    split = P(("user", "hist"))
    in_specs = (split, split, split, P("user"), split, split, split, P(), P(), P(), P())
    return jax.shard_map(body, mesh=mesh, in_specs=in_specs, out_specs=split, check_vma=False)
```

```python
import functools

import jax
import jax.numpy as jnp
from jax import lax
from jax.experimental import pallas as pl
from jax.experimental.pallas import tpu as pltpu
from jax.sharding import PartitionSpec as P

HEADS = 8
HEAD = 128
BLK = 128
BLK_USR = 16
USERS = 4
SLOTS = 32
CHUNK = 512
NOTE = 8
PAD = 16
SORTED = CHUNK + 128
COPY = 64
SHORT = 160
TILES = (256, 512, 768)
TILE = TILES[-1]
KEYS = 1024
UNIT = 512
VMEM = 48 * 1024 * 1024

BF16 = jnp.bfloat16
F32 = jnp.float32


def dot(a, b, contract):
    return lax.dot_general(a, b, ((contract[0], contract[1]), ((), ())), preferred_element_type=F32)


def silu(value):
    half = 0.5 * value
    return half + half * jnp.tanh(half)


def params():
    return pltpu.CompilerParams(vmem_limit_bytes=VMEM)


def vmem():
    return pl.BlockSpec(memory_space=pltpu.VMEM)


def smem():
    return pl.BlockSpec(memory_space=pltpu.SMEM)


def regroup_kernel(keys_ref, values_ref, out_ref):
    out_ref[0, :, :HEAD] = keys_ref[...]
    out_ref[0, :, HEAD:] = values_ref[...]


def regroup(keys, values):
    rows = keys.shape[0]
    return pl.pallas_call(
        regroup_kernel,
        grid=(HEADS,),
        out_shape=jax.ShapeDtypeStruct((HEADS, rows, 2 * HEAD), BF16),
        in_specs=[pl.BlockSpec((rows, HEAD), lambda h: (0, h))] * 2,
        out_specs=pl.BlockSpec((1, rows, 2 * HEAD), lambda h: (h, 0, 0)),
        compiler_params=params(),
        name="regroup",
    )(keys, values)


def query_kernel(
    turn_ref,
    list_hbm,
    group_hbm,
    user_hbm,
    embed_hbm,
    gain_hbm,
    w_hbm,
    packed_hbm,
    normed_ref,
    slot_ref,
    listed,
    group_ref,
    user_ref,
    embed_ref,
    gain_ref,
    w_ref,
    packed_ref,
    sems,
    w_sems,
    out_sems,
):
    rows = embed_ref.shape[0]
    groups = packed_hbm.shape[0]
    slots = groups * SLOTS
    steps, _, step = w_ref.shape
    fetches = [
        pltpu.make_async_copy(source, target, sems.at[i])
        for i, (source, target) in enumerate(
            (
                (group_hbm, group_ref),
                (user_hbm, user_ref),
                (embed_hbm, embed_ref),
                (gain_hbm, gain_ref),
                (list_hbm, listed),
            )
        )
    ]
    for fetch in fetches:
        fetch.start()
    blocks = [
        pltpu.make_async_copy(w_hbm.at[:, pl.ds(i * step, step)], w_ref.at[i], w_sems.at[i])
        for i in range(steps)
    ]
    for block in blocks:
        block.start()

    fetches[0].wait()
    group = group_ref[...]
    member = (group == lax.broadcasted_iota(jnp.int32, (groups, rows), 0)).astype(F32)
    before = (
        lax.broadcasted_iota(jnp.int32, (rows, rows), 0)
        < lax.broadcasted_iota(jnp.int32, (rows, rows), 1)
    ).astype(BF16)
    count = dot(member.astype(BF16), before, ((1,), (0,)))
    position = jnp.sum(count * member, axis=0, keepdims=True).astype(jnp.int32)
    slot = group * SLOTS + position
    slot_ref[...] = slot
    place = (slot == lax.broadcasted_iota(jnp.int32, (slots, rows), 0)).astype(BF16)
    fetches[1].wait()
    offset = turn_ref[0] * SLOTS
    lanes = lax.broadcasted_iota(jnp.int32, (HEAD, rows), 0) == position + offset
    users = member * (user_ref[...] - USERS).astype(F32)
    tags = dot(users.astype(BF16), lanes.astype(BF16), ((1,), (1,)))
    own = lax.broadcasted_iota(jnp.int32, tags.shape, 1) - offset
    tags = tags + jnp.where((own >= 0) & (own < SLOTS), USERS, 0).astype(F32)
    fetches[4].wait()
    lane = lax.broadcasted_iota(jnp.int32, (groups, NOTE, HEAD), 2)
    row = lax.broadcasted_iota(jnp.int32, (groups, NOTE, HEAD), 1)
    blocks_here = jnp.zeros((groups, NOTE, HEAD), jnp.int32)
    for b in range(list_hbm.shape[1]):
        blocks_here = jnp.where(lane == b, listed[0, b], blocks_here)
    tags = jnp.broadcast_to(tags.reshape(groups, 1, HEAD), (groups, NOTE, HEAD))
    notes = jnp.where(
        row == 0, tags, jnp.where(row == 1, blocks_here.astype(F32), 0.0)
    ).astype(BF16)

    fetches[2].wait()
    fetches[3].wait()
    values = embed_ref[...].astype(F32)
    scaling = lax.rsqrt(jnp.mean(values * values, axis=-1, keepdims=True) + 1e-06)
    normed = (values * scaling * gain_ref[...]).astype(BF16)
    normed_ref[...] = normed
    stores = []
    for i in range(steps):
        blocks[i].wait()
        query = dot(normed, w_ref[i], ((1,), (0,)))
        query = silu(query).astype(BF16)
        packed = dot(place, query, ((1,), (0,))).astype(BF16)
        for j in range(step // HEAD):
            h = i * (step // HEAD) + j
            packed_ref[h, :, :SLOTS] = packed[:, j * HEAD : (j + 1) * HEAD].reshape(
                groups, SLOTS, HEAD
            )
            packed_ref[h, :, SLOTS:] = notes
            store = pltpu.make_async_copy(packed_ref.at[h], packed_hbm.at[:, h], out_sems.at[h])
            store.start()
            stores.append(store)
    for store in stores:
        store.wait()


def make_queries(turn, listed, group, user, embed, gain, w_in, groups):
    rows, width = embed.shape
    step = 4 * HEAD
    hbm = pl.BlockSpec(memory_space=pltpu.HBM)
    return pl.pallas_call(
        query_kernel,
        out_shape=(
            jax.ShapeDtypeStruct((groups, HEADS, SLOTS + NOTE, HEAD), BF16),
            jax.ShapeDtypeStruct((rows, width), BF16),
            jax.ShapeDtypeStruct((1, rows), jnp.int32),
        ),
        in_specs=[smem()] + [hbm] * 6,
        out_specs=(hbm, vmem(), vmem()),
        scratch_shapes=[
            pltpu.SMEM(listed.shape, jnp.int32),
            pltpu.VMEM((1, rows), jnp.int32),
            pltpu.VMEM((1, rows), jnp.int32),
            pltpu.VMEM((rows, width), BF16),
            pltpu.VMEM((1, width), F32),
            pltpu.VMEM((width // step, width, step), BF16),
            pltpu.VMEM((HEADS, groups, SLOTS + NOTE, HEAD), BF16),
            pltpu.SemaphoreType.DMA((5,)),
            pltpu.SemaphoreType.DMA((width // step,)),
            pltpu.SemaphoreType.DMA((HEADS,)),
        ],
        compiler_params=pltpu.CompilerParams(vmem_limit_bytes=64 * 1024 * 1024),
        name="make_queries",
    )(turn, listed, group, user, embed, gain.reshape(1, width), w_in)


def gate_kernel(slot_ref, normed_ref, w_ref, gate_ref, place_ref):
    rows = normed_ref.shape[0]
    gate = dot(normed_ref[...], w_ref[...], ((1,), (0,)))
    gate_ref[...] = silu(gate).astype(BF16)
    column = jnp.broadcast_to(slot_ref[...].astype(F32), (8, rows)).T[:, :1].astype(jnp.int32)
    lane = lax.broadcasted_iota(jnp.int32, place_ref.shape, 1)
    place_ref[...] = (column == lane).astype(BF16)


def make_gate(slot, normed, w_in, slots):
    rows, width = normed.shape
    return pl.pallas_call(
        gate_kernel,
        grid=(1,),
        out_shape=(
            jax.ShapeDtypeStruct((rows, width), BF16),
            jax.ShapeDtypeStruct((rows, slots), BF16),
        ),
        in_specs=[
            pl.BlockSpec((1, rows), lambda i: (0, 0)),
            pl.BlockSpec((rows, width), lambda i: (0, 0)),
            pl.BlockSpec((width, width), lambda i: (0, 1)),
        ],
        out_specs=(
            pl.BlockSpec((rows, width), lambda i: (0, 0)),
            pl.BlockSpec((rows, slots), lambda i: (0, 0)),
        ),
        compiler_params=params(),
        name="make_gate",
    )(slot, normed, w_in)


def padded(count):
    return (count + (PAD - 1)) // PAD * PAD


def bases(counts_ref, chunks):
    starts, sizes, start = [], [], jnp.int32(0)
    for u in range(USERS):
        size = jnp.int32(0)
        for c in range(chunks):
            size = size + padded(counts_ref[c, u])
        starts.append(start)
        sizes.append(size)
        start = start + size
    return starts, sizes


def copy_rows(count, source, start, target, end):
    def step(i, carry):
        rows = source[pl.ds(pl.multiple_of(start + i * COPY, PAD), COPY), :]
        target[pl.ds(pl.multiple_of(end + i * COPY, PAD), COPY), :] = rows
        return carry

    lax.fori_loop(0, (count + (COPY - 1)) // COPY, step, 0)


def runs(counts_ref, c):
    starts, start = [], jnp.int32(0)
    for u in range(USERS):
        starts.append(start)
        start = start + padded(counts_ref[c, u])
    return starts


def sort_kernel(counts_ref, tags_ref, query_ref, pick_ref, sorted_ref, chunk_ref):
    chunks = tags_ref.shape[0]
    sources = CHUNK // SLOTS
    earlier = (
        lax.broadcasted_iota(jnp.int32, (CHUNK, CHUNK), 0)
        < lax.broadcasted_iota(jnp.int32, (CHUNK, CHUNK), 1)
    ).astype(BF16)
    places = []
    for c in range(chunks):
        tags = tags_ref[c : c + 1, :]
        lanes = (tags == lax.broadcasted_iota(jnp.int32, (8, CHUNK), 0)).astype(F32)
        rank = dot(lanes.astype(BF16), earlier, ((1,), (0,))).astype(jnp.int32)
        starts = runs(counts_ref, c)
        place = jnp.full((1, CHUNK), -1, jnp.int32)
        for u in range(USERS):
            place = jnp.where(tags == u, rank[u : u + 1, :] + starts[u], place)
        places.append(place)
        pick = (lax.broadcasted_iota(jnp.int32, (SORTED, CHUNK), 0) == place).astype(BF16)
        query = query_ref[c * sources : (c + 1) * sources, :SLOTS].reshape(CHUNK, HEAD)
        chunk_ref[c * SORTED : (c + 1) * SORTED, :] = dot(pick, query, ((1,), (0,))).astype(BF16)
    chunk_ref[chunks * SORTED :, :] = jnp.zeros((COPY, HEAD), BF16)
    sorted_ref[...] = jnp.zeros_like(sorted_ref)
    row = jnp.int32(0)
    for u in range(USERS):
        for c in range(chunks):
            count = counts_ref[c, u]
            copy_rows(count, chunk_ref, c * SORTED + runs(counts_ref, c)[u], sorted_ref, row)
            row = row + padded(count)
    columns = jnp.concatenate(places, axis=0).astype(F32).T.astype(jnp.int32)
    for c in range(chunks):
        lane = lax.broadcasted_iota(jnp.int32, (CHUNK, SORTED), 1)
        pick_ref[c] = (columns[:, c : c + 1] == lane).astype(BF16)


def sort_queries(counts, tags, query):
    chunks = tags.shape[0]
    return pl.pallas_call(
        sort_kernel,
        out_shape=(
            jax.ShapeDtypeStruct((chunks, CHUNK, SORTED), BF16),
            jax.ShapeDtypeStruct((chunks * SORTED + TILE, HEAD), BF16),
        ),
        in_specs=[smem(), vmem(), vmem()],
        out_specs=(vmem(), vmem()),
        scratch_shapes=[pltpu.VMEM((chunks * SORTED + COPY, HEAD), BF16)],
        compiler_params=params(),
        name="sort_queries",
    )(counts, tags, query)


def attend_kernel(
    counts_ref,
    where_ref,
    length_ref,
    query_ref,
    pick_hbm,
    kv_hbm,
    out_ref,
    kv,
    pick,
    total,
    start_ref,
    size_ref,
    kv_sem,
    pick_sem,
    *chunk,
):
    chunks = out_ref.shape[0]
    blocks = kv_hbm.shape[1] // BLK
    starts, sizes = bases(counts_ref, chunks)
    fetch = pltpu.make_async_copy(kv_hbm, kv, kv_sem)
    fetch.start()
    total[...] = jnp.zeros_like(total)
    for part in chunk:
        part[...] = jnp.zeros_like(part)
    fetch.wait()
    picks = pltpu.make_async_copy(pick_hbm, pick, pick_sem)
    picks.start()

    scale = 0.5 * HEAD ** (-0.5)

    def partial(query, u, first, count, limit):
        parts = []
        for j in range(count):
            at = where_ref[u * BLK_USR + first + j]
            row = pl.multiple_of(at % blocks * BLK, BLK)
            parts.append(kv[at // blocks, pl.ds(row, BLK), :])
        part = jnp.concatenate(parts, axis=0)
        half = dot(query, part[:, :HEAD], ((1,), (1,))) * scale
        weight = half + half * jnp.tanh(half)
        if limit is not None:
            column = lax.broadcasted_iota(jnp.int32, weight.shape, 1)
            weight = jnp.where(column < limit, weight, 0.0)
        return dot(weight.astype(BF16), part[:, HEAD:], ((1,), (0,)))

    def attend_tile(size, u, at):
        length = length_ref[u]
        units = (length + (UNIT - 1)) // UNIT
        whole = (units - 1) // (KEYS // UNIT)
        query = query_ref[pl.ds(at, size), :]

        def step(k, running):
            return running + partial(query, u, k * (KEYS // BLK), KEYS // BLK, None)

        running = lax.fori_loop(0, whole, step, jnp.zeros((size, HEAD), F32))
        first = whole * KEYS
        for count in range(1, KEYS // UNIT + 1):

            @pl.when(units - whole * (KEYS // UNIT) == count)
            def _(count=count):
                rest = partial(query, u, first // BLK, count * UNIT // BLK, length - first)
                total[pl.ds(at, size), :] = (running + rest).astype(BF16)

    for u in range(USERS):
        start_ref[u] = starts[u]
        size_ref[u] = sizes[u]

    def attend_user(u, carry):
        def attend_rows(state):
            at, left = state
            for shorter, size in zip((0,) + TILES[:-1], TILES):
                fits = left > shorter
                if size < TILE:
                    fits = fits & (left <= size)

                @pl.when(fits)
                def _(size=size):
                    attend_tile(size, u, pl.multiple_of(at, PAD))

            return at + TILE, left - TILE

        lax.while_loop(lambda state: state[1] > 0, attend_rows, (start_ref[u], size_ref[u]))
        return carry

    lax.fori_loop(0, USERS, attend_user, 0)

    picks.wait()
    rows = list(starts)
    moves = []
    short = True
    for c in range(chunks):
        run = runs(counts_ref, c)
        for u in range(USERS):
            count = counts_ref[c, u]
            moves.append((c, count, rows[u], run[u]))
            rows[u] = rows[u] + padded(count)
            short = short & (count <= SHORT)
        short = short & (run[USERS - 1] + padded(counts_ref[c, USERS - 1]) <= CHUNK)

    def put_back(size):
        for c in range(chunks):
            out_ref[c] = dot(pick[c, :, :size], chunk[c][:size, :], ((1,), (0,))).astype(BF16)

    @pl.when(short)
    def _():
        for c, _, source, target in moves:
            run = total[pl.ds(pl.multiple_of(source, PAD), SHORT), :]
            chunk[c][pl.ds(pl.multiple_of(target, PAD), SHORT), :] = run
        put_back(CHUNK)

    @pl.when(jnp.logical_not(short))
    def _():
        for c, count, source, target in moves:
            copy_rows(count, total, source, chunk[c], target)
        put_back(SORTED)


def attend(counts, where, length, query, pick, kv):
    chunks = pick.shape[0]
    rows = query.shape[0]
    anywhere = pl.BlockSpec(memory_space=pl.ANY)
    return pl.pallas_call(
        attend_kernel,
        out_shape=jax.ShapeDtypeStruct((chunks, CHUNK, HEAD), BF16),
        in_specs=[smem(), smem(), smem(), vmem(), anywhere, anywhere],
        out_specs=vmem(),
        scratch_shapes=[
            pltpu.VMEM(kv.shape, BF16),
            pltpu.VMEM(pick.shape, BF16),
            pltpu.VMEM((rows, HEAD), BF16),
            pltpu.SMEM((USERS,), jnp.int32),
            pltpu.SMEM((USERS,), jnp.int32),
            pltpu.SemaphoreType.DMA,
            pltpu.SemaphoreType.DMA,
        ]
        + [pltpu.VMEM((SORTED + SHORT, HEAD), BF16)] * chunks,
        compiler_params=params(),
        name="attend",
    )(counts, where, length, query, pick, kv)


def finish_kernel(returned_ref, place_ref, embed_ref, gate_ref, gain_ref, w_ref, out_ref):
    slots = place_ref.shape[1]
    returned = [returned_ref[:, h].reshape(slots, HEAD) for h in range(HEADS)]
    picked = dot(place_ref[...], jnp.concatenate(returned, axis=1), ((1,), (0,)))
    scaling = lax.rsqrt(jnp.mean(picked * picked, axis=-1, keepdims=True) + 1e-05)
    gated = (picked * scaling * gain_ref[...] * gate_ref[...].astype(F32)).astype(BF16)
    mixed = embed_ref[...].astype(F32) + dot(gated, w_ref[...], ((1,), (0,)))
    out_ref[...] = mixed.astype(BF16)


def finish(returned, place, embed, gate, gain, w_out):
    rows, width = embed.shape
    return pl.pallas_call(
        finish_kernel,
        out_shape=jax.ShapeDtypeStruct((rows, width), BF16),
        in_specs=[vmem()] * 6,
        out_specs=vmem(),
        compiler_params=params(),
        name="finish",
    )(returned, place, embed, gate, gain.reshape(1, width), w_out)


def body(
    cand_embed,
    cand_group,
    cand_user,
    hist_len,
    block_list,
    hist_keys,
    hist_values,
    in_gain,
    w_in,
    attn_gain,
    w_out,
):
    groups = lax.axis_size("user")
    hist_count = lax.axis_size("hist")
    devices = groups * hist_count
    everyone = ("user", "hist")
    blocks_here = block_list.shape[0]

    rows = cand_embed.shape[0]
    me_user = lax.axis_index("user")
    me = me_user * hist_count + lax.axis_index("hist")
    turn = jnp.reshape(me % (HEAD // SLOTS), (1,)).astype(jnp.int32)
    packed, normed, slot = make_queries(
        turn,
        block_list.reshape(1, -1),
        cand_group.reshape(1, rows),
        cand_user.reshape(1, rows),
        cand_embed,
        in_gain,
        w_in,
        groups,
    )
    packed, keys, values, normed = lax.optimization_barrier(
        (packed, hist_keys, hist_values, normed)
    )
    arrived = lax.all_to_all(
        packed.reshape(devices, SLOTS + NOTE, HEAD),
        everyone,
        split_axis=0,
        concat_axis=0,
        tiled=True,
    )
    kv = regroup(keys, values)
    gate, place = make_gate(slot, normed, w_in, groups * SLOTS)
    kv, arrived, gate, place = lax.optimization_barrier((kv, arrived, gate, place))
    kv = lax.all_to_all(kv, "hist", split_axis=0, concat_axis=0, tiled=True)

    tags = arrived[:, SLOTS, :].astype(jnp.int32).reshape(-1, HEAD // SLOTS, HEAD)
    tags = jnp.sum(tags, axis=1).reshape(devices * SLOTS // CHUNK, CHUNK)
    counts = jnp.sum(
        tags[:, None, :] == jnp.arange(USERS, dtype=jnp.int32)[None, :, None],
        axis=2,
        dtype=jnp.int32,
    )
    listed = lax.dynamic_slice(
        arrived, (me_user * hist_count, SLOTS + 1, 0), (hist_count, 1, blocks_here)
    )
    listed = listed.astype(jnp.int32).reshape(1, -1)
    order = jnp.arange(hist_count * blocks_here, dtype=jnp.int32)
    where = jnp.sum(jnp.where(listed == order[:, None], order[None, :], 0), axis=1)
    pick, query = sort_queries(counts, tags, arrived)

    attended = attend(counts, where, hist_len, query, pick, kv)
    returned = lax.all_to_all(
        attended.reshape(devices, SLOTS, HEAD), everyone, split_axis=0, concat_axis=0, tiled=True
    )
    return finish(
        returned.reshape(groups, HEADS, SLOTS, HEAD), place, cand_embed, gate, attn_gain, w_out
    )


def solution(mesh):
    split = P(("user", "hist"))
    in_specs = (split, split, split, P("user"), split, split, split, P(), P(), P(), P())
    return jax.shard_map(body, mesh=mesh, in_specs=in_specs, out_specs=split, check_vma=False)
```
